512 devices in a mesh: blk: 64 (over x, y, z_hi), edge: 8 (over z_lo, core).
Axes of the slice: x: 4, y: 8, z: 8 (z_hi: 2, z_lo: 4; z = z_hi * 4 + z_lo), core: 2. Of those that a mesh axis runs over, the one named last changes fastest.
Arguments:
- node_feat: bfloat16 [8192, 128], P(('blk', 'edge')), may hold values from -6 to 6
- coords: bfloat16 [3, 8192], P(None, ('blk', 'edge')), may hold values from -4 to 4
- pair_table: int32 [3, 64], replicated, may hold values from 0 to 63, as said below
- w_tgt: bfloat16 [128, 128], replicated, may hold values from -0.375 to 0.375
- w_src: bfloat16 [128, 128], replicated, may hold values from -0.375 to 0.375
- w_dist: float32 [128], replicated, may hold values from -0.8 to 0.8
- edge_bias: float32 [128], replicated, may hold values from -2 to 2
- w_edge: bfloat16 [128, 128], replicated, may hold values from -0.5 to 0.5
- w_gate: float32 [128], replicated, may hold values from -1.5 to 1.5
- w_coord: bfloat16 [128, 128], replicated, may hold values from -0.5 to 0.5
- w_weight: float32 [128], replicated, may hold values from -5 to 5
- w_node_in: bfloat16 [256, 128], replicated, may hold values from -0.375 to 0.375
- w_node_out: bfloat16 [128, 128], replicated, may hold values from -0.5 to 0.5
Outputs:
- new_feat: bfloat16 [8192, 128], P(('blk', 'edge'))
- new_coords: float32 [3, 8192], P(None, ('blk', 'edge'))
The draws below stay inside these ranges and needn't reach their ends.
Inputs may be any that keep to these rules, and one draw needn't show every extreme that they name: Each row pairs the 64 blocks: pair_table[r, b] = c exactly when pair_table[r, c] = b, and c is never b; no block meets the same partner in two rows.
All inputs are finite; a program needn't handle non-finite values.
Results may differ from the reference program's by a relative error of at most 0.0027.
Values may be sent and summed in bfloat16 or wider, within the bound.
A program may use at most 128 MiB of HBM per device.

```python
import jax
import jax.numpy as jnp
from jax import lax

F = 128
ROUNDS = 3
BLOCKS = 64
NODES = 8192


def draw_pair_table(key, part):
    label_order = jax.random.permutation(jax.random.fold_in(key, 11), BLOCKS).astype(jnp.int32)
    round_labels = jax.random.permutation(jax.random.fold_in(key, 12), BLOCKS - 1)[:ROUNDS].astype(jnp.int32)
    label_of = jnp.zeros((BLOCKS,), jnp.int32).at[label_order].set(jnp.arange(BLOCKS, dtype=jnp.int32))
    last_label = BLOCKS - 1
    own_label = label_of[None, :]
    round_label = round_labels[:, None]
    mirrored = jnp.mod(2 * round_label - own_label, last_label)
    partner_label = jnp.where(own_label == last_label, round_label, jnp.where(own_label == round_label, last_label, mirrored))
    return label_order[partner_label].astype(jnp.int32)


def shard_levels(key, shape, pieces, least, largest):
    gain, own = 1.0, jax.random.fold_in(key, 6)
    for dim, shards_of in pieces:
        draws = jnp.exp(jax.random.uniform(jax.random.fold_in(own, dim), (shards_of,), jnp.float32, least / len(pieces), largest / len(pieces)))
        gain = gain * jnp.repeat(draws, shape[dim] // shards_of).reshape([-1 if axis == dim else 1 for axis in range(len(shape))])
    return gain


def normal_values(rng, extent, width, bound, split=(), kind=jnp.bfloat16):
    array = jax.random.normal(rng, extent, jnp.float32) * width
    if len(split) > 0:
        array = shard_levels(rng, extent, split, -0.22, 0.18) * array
    return jnp.clip(array, min=-bound, max=bound).astype(kind)


def setup_inputs(seed: int = 0) -> dict:
    arg_keys = jax.random.split(jax.random.key(seed), 14)
    node_feat = normal_values(arg_keys[0], (NODES, F), 1.0, 6.0, ((0, 512),))
    coords = normal_values(arg_keys[1], (3, NODES), 1.0, 4.0, ((1, 512),))
    pair_table = draw_pair_table(jax.random.fold_in(arg_keys[13], 71), 0)
    w_tgt = normal_values(arg_keys[3], (F, F), (2 * F) ** -0.5, 0.375)
    w_src = normal_values(arg_keys[4], (F, F), (2 * F) ** -0.5, 0.375)
    w_dist = normal_values(arg_keys[5], (F,), 0.2, 0.8, (), jnp.float32)
    edge_bias = normal_values(arg_keys[6], (F,), 0.5, 2.0, (), jnp.float32)
    w_edge = normal_values(arg_keys[7], (F, F), F ** -0.5, 0.5)
    w_gate = normal_values(arg_keys[8], (F,), 16 ** -0.5, 1.5, (), jnp.float32)
    w_coord = normal_values(arg_keys[9], (F, F), F ** -0.5, 0.5)
    w_weight = normal_values(arg_keys[10], (F,), 1.0, 5.0, (), jnp.float32)
    w_node_in = normal_values(arg_keys[11], (2 * F, F), (2 * F) ** -0.5, 0.375)
    w_node_out = normal_values(arg_keys[12], (F, F), F ** -0.5, 0.5)
    return dict(node_feat=node_feat, coords=coords, pair_table=pair_table, w_tgt=w_tgt, w_src=w_src, w_dist=w_dist, edge_bias=edge_bias, w_edge=w_edge, w_gate=w_gate, w_coord=w_coord, w_weight=w_weight, w_node_in=w_node_in, w_node_out=w_node_out)


def edge_terms(tgt_proj, tgt_place, src_feat, src_place, keep_mask, w_src, w_dist, edge_bias, w_edge, w_gate, w_coord, w_weight):
    src_proj = jnp.dot(src_feat, w_src, preferred_element_type=jnp.float32)
    offset = tgt_place.astype(jnp.float32)[:, :, None] - src_place.astype(jnp.float32)[:, None, :]
    radial = lax.optimization_barrier(jnp.sum(offset * offset, axis=0))
    targets = radial.shape[0]
    sources = radial.shape[1]
    pre_act = tgt_proj[:, None, :] + src_proj[None, :, :] + radial[:, :, None] * w_dist + edge_bias
    hidden = jax.nn.silu(pre_act).astype(jnp.bfloat16).reshape(targets * sources, -1)
    message = jax.nn.silu(jnp.dot(hidden, w_edge, preferred_element_type=jnp.float32))
    edge_gate = jax.nn.sigmoid(lax.optimization_barrier(jnp.sum(message * w_gate, axis=1))).reshape(targets, sources) * keep_mask
    lifted = jax.nn.silu(jnp.dot(message.astype(jnp.bfloat16), w_coord, preferred_element_type=jnp.float32))
    weight = lax.optimization_barrier(jnp.sum(lifted * w_weight, axis=1)).reshape(targets, sources) * keep_mask
    message_sum = lax.optimization_barrier(jnp.sum(message.reshape(targets, sources, -1) * edge_gate[:, :, None], axis=1))
    unit_dir = offset / (jnp.sqrt(radial) + 1.0)
    coord_sum = lax.optimization_barrier(jnp.sum(unit_dir * weight[None], axis=2))
    return (message_sum, coord_sum)

def reference(node_feat, coords, pair_table, w_tgt, w_src, w_dist, edge_bias, w_edge, w_gate, w_coord, w_weight, w_node_in, w_node_out):
    blocks = pair_table.shape[1]
    rounds = pair_table.shape[0]
    feat_width = node_feat.shape[1]
    block_size = node_feat.shape[0] // blocks
    feat_blocks = node_feat.reshape(blocks, block_size, feat_width)
    place_blocks = coords.reshape(3, blocks, block_size).transpose(1, 0, 2)
    mean_scale = 1.0 / ((rounds + 1) * block_size - 1)
    inner_ids = jnp.arange(block_size, dtype=jnp.int32)
    self_keep = (inner_ids[:, None] != inner_ids[None, :]).astype(jnp.float32)
    all_keep = jnp.ones((block_size, block_size), jnp.float32)
    weights = (w_src, w_dist, edge_bias, w_edge, w_gate, w_coord, w_weight)

    def one_block(block_index):
        block_feat = feat_blocks[block_index]
        block_place = place_blocks[block_index]
        tgt_proj = jnp.dot(block_feat, w_tgt, preferred_element_type=jnp.float32)
        message_sum, coord_sum = edge_terms(tgt_proj, block_place, block_feat, block_place, self_keep, *weights)
        for round_step in range(rounds):
            partner = pair_table[round_step, block_index]
            more_msg, more_coord = edge_terms(tgt_proj, block_place, feat_blocks[partner], place_blocks[partner], all_keep, *weights)
            message_sum = message_sum + more_msg
            coord_sum = coord_sum + more_coord
        message_mean = (message_sum * mean_scale).astype(jnp.bfloat16)
        node_pre = jnp.dot(block_feat, w_node_in[:feat_width], preferred_element_type=jnp.float32) + jnp.dot(message_mean, w_node_in[feat_width:], preferred_element_type=jnp.float32)
        node_hidden = jax.nn.silu(node_pre).astype(jnp.bfloat16)
        new_block = (block_feat.astype(jnp.float32) + jnp.dot(node_hidden, w_node_out, preferred_element_type=jnp.float32)).astype(jnp.bfloat16)
        new_place = block_place.astype(jnp.float32) + coord_sum * mean_scale
        return (new_block, new_place)
    new_blocks, new_places = lax.map(one_block, jnp.arange(blocks, dtype=jnp.int32))
    return (new_blocks.reshape(-1, feat_width), new_places.transpose(1, 0, 2).reshape(3, -1))
```

```python
import functools

import jax
import jax.numpy as jnp
from jax import lax
from jax.experimental import pallas as pl
from jax.experimental.pallas import tpu as pltpu
from jax.sharding import PartitionSpec as P

MESH = pl.DeviceIdType.MESH
F32 = jnp.float32
BF16 = jnp.bfloat16

NX, NY, NZ = 4, 8, 8
RING = {4: (2, 1, 3, 0), 8: (4, 3, 5, 2, 6, 1, 7, 0)}
PLANE = [(dx, dy) for dx in RING[NX] for dy in RING[NY] if dx or dy]
COLUMN = [(dz, dc) for dz in RING[NZ] for dc in (1, 0) if dz or dc]
EDGE = (4, 3, 5, 2, 6, 1, 7)
ROWS = 16
TERMS = 16


def iota(shape, dim):
    return lax.broadcasted_iota(jnp.int32, shape, dim)


def dot(a, b, dims=((1,), (0,))):
    return lax.dot_general(a, b, (dims, ((), ())), preferred_element_type=F32)


def split2(a):
    high = a.astype(BF16)
    return high, (a - high.astype(F32)).astype(BF16)


def half_silu(h):
    return h + h * jnp.tanh(h)


def source_rows(places, count):
    slots = places.shape[0]
    lane = iota((128, count), 0)
    node = lax.rem(iota((128, count), 1), 16)
    mine = (iota((slots, count), 1) // 16) == iota((slots, count), 0)
    low = places.astype(BF16)
    rows = []
    for k in range(3):
        spread = dot(low, (lane == node + 16 * k).astype(BF16))
        rows.append(jnp.sum(jnp.where(mine, spread, 0.0), axis=0, keepdims=True))
    return rows


def edge_sums(lhs_ref, base, count, places, own, target_cols, wide_ref, w_edge2, w_coord2, gate_row, weight_row):
    rows = source_rows(places, count)
    norm = rows[0] * rows[0] + rows[1] * rows[1] + rows[2] * rows[2]
    norm_high, norm_mid = split2(norm)
    norm_low = (norm - norm_high.astype(F32) - norm_mid.astype(F32)).astype(F32)
    one = jnp.ones((1, count), F32)
    nh, nm = norm_high.astype(F32), norm_mid.astype(F32)
    terms = rows + rows + [nh, nm, nh, one, one, norm_low]
    terms = jnp.concatenate(terms + [jnp.zeros((TERMS - len(terms), count), F32)], axis=0).astype(BF16)
    place_term = (iota((TERMS, 128), 0) == iota((TERMS, 128), 1)).astype(BF16)
    lhs_ref[pl.ds(base, count), 128:256] = dot(terms, place_term, ((0,), (0,))).astype(BF16)
    lhs = lhs_ref[pl.ds(base, count), :]

    offsets = [target_cols[k][:, :1] - rows[k] for k in range(3)]
    radial = offsets[0] * offsets[0] + offsets[1] * offsets[1] + offsets[2] * offsets[2]
    scale = 1.0 / (jnp.sqrt(radial) + 1.0)

    row16, col16 = iota((16, 256), 0), iota((16, 256), 1)
    message_sum = jnp.zeros((16, 256), F32)
    weights = jnp.zeros((16, count), F32)
    for pair in range(8):
        half = dot(lhs, wide_ref[pair]).astype(BF16)
        hidden = half_silu(half)
        message = half_silu(dot(hidden, w_edge2).astype(BF16))
        lifted = half_silu(dot(message, w_coord2).astype(BF16))
        here = row16 == 2 * pair + col16 // 128
        pick = lambda pieces: jnp.concatenate([jnp.where(here, p, 0.0) for p in pieces], axis=0).astype(BF16)
        logit = dot(pick(gate_row), message, ((1,), (1,)))
        gate = 0.5 + 0.5 * jnp.tanh(logit[:16] + logit[16:])
        if own is not None:
            gate = gate * own
        message_sum = message_sum + jnp.where(here, dot(gate.astype(BF16), message), 0.0)
        weight = dot(pick(weight_row), lifted, ((1,), (1,)))
        weights = weights + (weight[:16] + weight[16:])
    if own is not None:
        weights = weights * own
    weights = weights * scale
    coord_sum = [jnp.sum(offsets[k] * weights, axis=1, keepdims=True) for k in range(3)]
    return message_sum[:, :128] + message_sum[:, 128:], coord_sum


def layer(
    feat_hbm, place_hbm, table_hbm, w_tgt_hbm, w_src_hbm, w_dist_hbm, bias_hbm, w_edge_hbm, w_gate_hbm,
    w_coord_hbm, w_weight_hbm, w_in_hbm, w_out_hbm,
    feat_out, place_out,
    feat, place, table, w_tgt, w_src, w_dist, bias, w_edge, w_gate, w_coord, w_weight, w_in, w_out,
    place_row, near_feat, near_place, plane_feat, plane_place, picked_feat, picked_place,
    column_feat, column_place, lhs, place_list, wide, edge_wide, coord_wide,
    load_sem, send_sem, recv_sem,
):
    blk, edge = lax.axis_index("blk"), lax.axis_index("edge")
    x, y, z_hi = blk // 16, (blk // 2) % 8, blk % 2
    core = edge % 2
    z = z_hi * 4 + edge // 2
    here = x * 8 + y
    spot = z * 2 + core

    plane = [{"blk": (lax.rem(x + dx, NX) * NY + lax.rem(y + dy, NY)) * 2 + z_hi} for dx, dy in PLANE]
    column = []
    for dz, dc in COLUMN:
        z_to = lax.rem(z + dz, NZ)
        column.append(({"blk": here * 2 + z_to // 4, "edge": (z_to % 4) * 2 + lax.rem(core + dc, 2)}, z_to // 4))
    near = [{"edge": lax.rem(edge + step, 8)} for step in EDGE]

    barrier = pltpu.get_barrier_semaphore()
    for peer in plane + [c[0] for c in column]:
        pl.semaphore_signal(barrier, inc=1, device_id=peer, device_id_type=MESH)
    loads = [
        pltpu.make_async_copy(a, b, load_sem.at[k])
        for k, (a, b) in enumerate(
            [
                (feat_hbm, feat), (place_hbm, place), (table_hbm, table), (w_tgt_hbm, w_tgt), (w_src_hbm, w_src),
                (w_dist_hbm, w_dist), (bias_hbm, bias), (w_edge_hbm, w_edge), (w_gate_hbm, w_gate),
                (w_coord_hbm, w_coord), (w_weight_hbm, w_weight), (w_in_hbm, w_in), (w_out_hbm, w_out),
            ]
        )
    ]
    for copy in loads:
        copy.start()
    loads[0].wait()
    loads[1].wait()
    places = place[...]
    row = jnp.zeros((1, 128), F32)
    for k in range(3):
        row = row + dot(places[k : k + 1], (iota((16, 128), 0) + 16 * k == iota((16, 128), 1)).astype(BF16))
    place_row[...] = row
    pl.semaphore_wait(barrier, len(plane) + len(column))

    def send(source, target, k, peer):
        pltpu.make_async_remote_copy(
            source, target, send_sem.at[k], recv_sem.at[k], device_id=peer, device_id_type=MESH
        ).start()

    def wait(buffer, count, semaphore):
        part = buffer.at[pl.ds(0, count)]
        pltpu.make_async_copy(part, part, semaphore).wait()

    for peer in plane:
        send(feat, plane_feat.at[here], 0, peer)
        send(place_row, plane_place.at[here], 1, peer)
    for peer in near:
        send(feat, near_feat.at[edge], 2, peer)
        send(place_row, near_place.at[edge], 3, peer)
    plane_feat[here] = feat[...]
    plane_place[here] = row
    near_feat[edge] = feat[...]
    near_place[edge] = row

    for copy in loads[2:]:
        copy.wait()
    own_feat = feat[...]
    cols = [
        dot(places, (iota((3, 128), 0) == k).astype(BF16), ((0,), (0,))) for k in range(3)
    ]
    own_norm = cols[0] * cols[0] + cols[1] * cols[1] + cols[2] * cols[2]
    dist = w_dist[...]
    base = 0.5 * (dot(own_feat, w_tgt[...]) + bias[...] + own_norm * dist)
    cross = [split2(-c * dist) for c in cols]
    dist_high, dist_mid = split2(jnp.broadcast_to(0.5 * dist, (16, 128)))
    base_high, base_mid = split2(base)
    stack = [c[0] for c in cross] + [c[1] for c in cross]
    stack += [dist_high, dist_high, dist_mid, base_high, base_mid, dist_high]
    stack = jnp.concatenate(stack + [jnp.zeros((16, 128), BF16)] * (TERMS - len(stack)), axis=0)
    to, of = iota((256, 256), 0), iota((256, 256), 1)
    turned = dot((of == (to % 16) * 16 + to // 16).astype(BF16), stack).astype(BF16)
    src_half = w_src[...] * jnp.asarray(0.5, BF16)
    none = jnp.zeros((128, 128), BF16)
    for pair in range(8):
        wide[pair, :128, :128] = src_half
        wide[pair, :128, 128:] = src_half
        for side in range(2):
            at = (2 * pair + side) * 16
            wide[pair, 128:144, side * 128 : side * 128 + 128] = turned[at : at + 16]
        wide[pair, 144:, :] = jnp.zeros((112, 256), BF16)
    for full, part in ((edge_wide, w_edge), (coord_wide, w_coord)):
        halved = part[...] * jnp.asarray(0.5, BF16)
        full[:128, :128] = halved
        full[128:, 128:] = halved
        full[:128, 128:] = none
        full[128:, :128] = none

    def pieces(vector, factor):
        high, mid = split2(jnp.concatenate([vector * factor] * 2, axis=1))
        return high.astype(F32), mid.astype(F32)

    gate_row = pieces(w_gate[...], 0.5)
    weight_row = pieces(w_weight[...], 1.0)
    shared = (cols, wide, edge_wide[...], coord_wide[...], gate_row, weight_row)

    wait(near_feat, 7, recv_sem.at[2])
    wait(near_place, 7, recv_sem.at[3])
    for k in range(8):
        lhs[k * 16 : k * 16 + 16, :128] = near_feat[k]
        place_list[k : k + 1, :] = near_place[k]
    keep = (iota((16, 128), 1) != edge * 16 + iota((16, 128), 0)).astype(F32)
    message_own, coord_own = edge_sums(lhs, 0, 128, place_list[0:8, :], keep, *shared)

    wait(plane_feat, 31, recv_sem.at[0])
    wait(plane_place, 31, recv_sem.at[1])
    for side in range(2):
        for r in range(3):
            from_spot = table[r, here * 2 + side] // 2
            picked_feat[side, r] = plane_feat[from_spot]
            picked_place[side, r] = plane_place[from_spot]
    for peer, side in column:
        send(picked_feat.at[side], column_feat.at[spot], 4, peer)
        send(picked_place.at[side], column_place.at[spot], 5, peer)
    column_feat[spot] = picked_feat[z_hi]
    column_place[spot] = picked_place[z_hi]
    wait(column_feat, 15, recv_sem.at[4])
    wait(column_place, 15, recv_sem.at[5])
    for r in range(3):
        side = table[r, blk] % 2
        for k in range(8):
            at = r * 8 + k
            lhs[at * 16 : at * 16 + 16, :128] = column_feat[side * 8 + k, r]
            place_list[at : at + 1, :] = column_place[side * 8 + k, r]
    message_far, coord_far = edge_sums(lhs, 0, 384, place_list[...], None, *shared)

    mean_scale = 1.0 / 511
    mean = ((message_own + message_far) * mean_scale).astype(BF16)
    node_pre = dot(own_feat, w_in[:128, :]) + dot(mean, w_in[128:, :])
    node_hidden = (node_pre * jax.nn.sigmoid(node_pre)).astype(BF16)
    feat_out[...] = (own_feat.astype(F32) + dot(node_hidden, w_out[...])).astype(BF16)
    eye = iota((16, 16), 0) == iota((16, 16), 1)
    for k in range(3):
        moved = jnp.sum(jnp.where(eye, coord_own[k] + coord_far[k], 0.0), axis=0, keepdims=True)
        place_out[k : k + 1, :] = places[k : k + 1].astype(F32) + mean_scale * moved

    for k, buffer, count in (
        (0, plane_feat, 31), (1, plane_place, 31), (2, near_feat, 7), (3, near_place, 7),
        (4, column_feat, 15), (5, column_place, 15),
    ):
        wait(buffer, count, send_sem.at[k])


def shards(*args):
    args = [a.reshape(1, -1) if a.ndim == 1 else a for a in args]
    vmem = lambda shape, kind: pltpu.VMEM(shape, kind)
    loaded = [
        pltpu.SMEM(a.shape, a.dtype) if a.dtype == jnp.int32 else pltpu.VMEM(a.shape, a.dtype) for a in args
    ]
    return pl.pallas_call(
        layer,
        out_shape=(jax.ShapeDtypeStruct((ROWS, 128), BF16), jax.ShapeDtypeStruct((3, ROWS), F32)),
        in_specs=[pl.BlockSpec(memory_space=pl.ANY)] * len(args),
        out_specs=(pl.BlockSpec(memory_space=pltpu.VMEM), pl.BlockSpec(memory_space=pltpu.VMEM)),
        scratch_shapes=loaded
        + [
            vmem((1, 128), F32),
            vmem((8, 16, 128), BF16),
            vmem((8, 1, 128), F32),
            vmem((32, 16, 128), BF16),
            vmem((32, 1, 128), F32),
            vmem((2, 3, 16, 128), BF16),
            vmem((2, 3, 1, 128), F32),
            vmem((16, 3, 16, 128), BF16),
            vmem((16, 3, 1, 128), F32),
            vmem((384, 256), BF16),
            vmem((24, 128), F32),
            vmem((8, 256, 256), BF16),
            vmem((256, 256), BF16),
            vmem((256, 256), BF16),
            pltpu.SemaphoreType.DMA((13,)),
            pltpu.SemaphoreType.DMA((6,)),
            pltpu.SemaphoreType.DMA((6,)),
        ],
        compiler_params=pltpu.CompilerParams(
            collective_id=0, has_side_effects=True, vmem_limit_bytes=48 * 1024 * 1024
        ),
    )(*args)


def solution(mesh):
    specs = (P(("blk", "edge"), None), P(None, ("blk", "edge"))) + (P(),) * 11
    return jax.shard_map(
        shards,
        mesh=mesh,
        in_specs=specs,
        out_specs=(P(("blk", "edge"), None), P(None, ("blk", "edge"))),
        check_vma=False,
    )
```

```python
import functools

import jax
import jax.numpy as jnp
from jax import lax
from jax.experimental import pallas as pl
from jax.experimental.pallas import tpu as pltpu
from jax.sharding import PartitionSpec as P

MESH = pl.DeviceIdType.MESH
F32 = jnp.float32
BF16 = jnp.bfloat16

NX, NY, NZ = 4, 8, 8
RING = {4: (2, 1, 3, 0), 8: (4, 3, 5, 2, 6, 1, 7, 0)}
PLANE = [(dx, dy) for dx in RING[NX] for dy in RING[NY] if dx or dy]
COLUMN = [(dz, dc) for dz in RING[NZ] for dc in (1, 0) if dz or dc]
EDGE = (4, 3, 5, 2, 6, 1, 7)
ROWS = 16
TERMS = 32


def iota(shape, dim):
    return lax.broadcasted_iota(jnp.int32, shape, dim)


def dot(a, b, dims=((1,), (0,))):
    return lax.dot_general(a, b, (dims, ((), ())), preferred_element_type=F32)


def split2(a):
    high = a.astype(BF16)
    return high, (a - high.astype(F32)).astype(BF16)


def half_silu(h):
    return h + h * jnp.tanh(h)


def place_terms(places, count):
    slots = places.shape[0]
    spread = jnp.broadcast_to(places[:, None, :], (slots, 16, 128)).reshape(count, 128)
    lane, node = iota((count, 128), 1), lax.rem(iota((count, 128), 0), 16)
    spread = jnp.where(lax.rem(lane, 16) == node, spread, 0.0)
    square_high, square_low = split2(spread * spread)
    parts = jnp.concatenate([spread.astype(BF16), square_high, square_low], axis=1)
    row, term = iota((384, 128), 0), iota((384, 128), 1)
    axis = lax.rem(row, 128) // 16
    kind = row // 128
    first = jnp.where(kind == 0, 0, 6 * kind)
    hit = (term == first + axis) | ((kind < 2) & (term == first + 3 + axis))
    placed = dot(parts, ((axis < 3) & hit).astype(BF16))
    ones = (lane == 15) | (lane == 16)
    return jnp.where(ones, 1.0, placed).astype(BF16)


def edge_sums(feats, places, count, own, target_cols, wide, w_edge2, w_coord2, gate_pick, weight_pick, hidden, message, lifted):
    terms = place_terms(places, count)
    chunks = [(at, pair) for pair in range(8) for at in range(0, count, 128)]
    lhs = [jnp.concatenate([feats(at), terms[at : at + 128]], axis=1) for at in range(0, count, 128)]
    for at, pair in chunks:
        half = dot(lhs[at // 128], wide[pair]).astype(BF16)
        hidden[at : at + 128, pair * 256 : pair * 256 + 256] = half_silu(half)

    rows8 = dot((iota((8, 128), 0) == iota((8, 128), 1)).astype(BF16), terms, ((1,), (1,)))
    offsets = [target_cols[k][:, :1] - rows8[k : k + 1] for k in range(3)]
    radial = offsets[0] * offsets[0] + offsets[1] * offsets[1] + offsets[2] * offsets[2]
    scale = 1.0 / (jnp.sqrt(radial) + 1.0)

    for at, pair in chunks:
        half = dot(hidden[at : at + 128, pair * 256 : pair * 256 + 256], w_edge2).astype(BF16)
        message[at : at + 128, pair * 256 : pair * 256 + 256] = half_silu(half)
    for at, pair in chunks:
        half = dot(message[at : at + 128, pair * 256 : pair * 256 + 256], w_coord2).astype(BF16)
        lifted[at : at + 128, pair * 256 : pair * 256 + 256] = half_silu(half)
    messages = message[:count, :]
    logit = dot(gate_pick[...], messages, ((1,), (1,)))
    gate = 0.5 + 0.5 * jnp.tanh(logit[:16] + logit[16:])
    weight = dot(weight_pick[...], lifted[:count, :], ((1,), (1,)))
    weight = (weight[:16] + weight[16:]) * scale
    if own is not None:
        gate, weight = gate * own, weight * own
    spread = dot(gate.astype(BF16), messages)
    row = iota((16, 128), 0)
    message_sum = jnp.zeros((16, 128), F32)
    for i in range(16):
        message_sum = message_sum + jnp.where(row == i, spread[:, i * 128 : i * 128 + 128], 0.0)
    coord_sum = [jnp.sum(offsets[k] * weight, axis=1, keepdims=True) for k in range(3)]
    return message_sum, coord_sum


def layer(
    feat_hbm, place_hbm, table_hbm, w_tgt_hbm, w_src_hbm, w_dist_hbm, bias_hbm, w_edge_hbm, w_gate_hbm,
    w_coord_hbm, w_weight_hbm, w_in_hbm, w_out_hbm,
    feat_out, place_out,
    feat, place, table, w_tgt, w_src, w_dist, bias, w_edge, w_gate, w_coord, w_weight, w_in, w_out,
    place_row, near_feat, near_place, plane_feat, plane_place, picked_feat, picked_place,
    column_feat, column_place, lhs, place_list, wide, edge_wide, coord_wide, gate_pick, weight_pick,
    hidden, message, lifted,
    load_sem, send_sem, recv_sem,
):
    blk, edge = lax.axis_index("blk"), lax.axis_index("edge")
    x, y, z_hi = blk // 16, (blk // 2) % 8, blk % 2
    core = edge % 2
    z = z_hi * 4 + edge // 2
    here = x * 8 + y
    spot = z * 2 + core

    plane = [{"blk": (lax.rem(x + dx, NX) * NY + lax.rem(y + dy, NY)) * 2 + z_hi} for dx, dy in PLANE]
    column = []
    for dz, dc in COLUMN:
        z_to = lax.rem(z + dz, NZ)
        column.append(({"blk": here * 2 + z_to // 4, "edge": (z_to % 4) * 2 + lax.rem(core + dc, 2)}, z_to // 4))
    near = [{"edge": lax.rem(edge + step, 8)} for step in EDGE]

    barrier = pltpu.get_barrier_semaphore()
    for peer in plane + [c[0] for c in column]:
        pl.semaphore_signal(barrier, inc=1, device_id=peer, device_id_type=MESH)
    loads = [
        pltpu.make_async_copy(a, b, load_sem.at[k])
        for k, (a, b) in enumerate(
            [
                (feat_hbm, feat), (place_hbm, place), (table_hbm, table), (w_tgt_hbm, w_tgt), (w_src_hbm, w_src),
                (w_dist_hbm, w_dist), (bias_hbm, bias), (w_edge_hbm, w_edge), (w_gate_hbm, w_gate),
                (w_coord_hbm, w_coord), (w_weight_hbm, w_weight), (w_in_hbm, w_in), (w_out_hbm, w_out),
            ]
        )
    ]
    for copy in loads:
        copy.start()
    loads[0].wait()
    loads[1].wait()
    places = place[...]
    row = jnp.zeros((1, 128), F32)
    for k in range(3):
        row = row + dot(places[k : k + 1], (iota((16, 128), 0) + 16 * k == iota((16, 128), 1)).astype(BF16))
    place_row[...] = row
    pl.semaphore_wait(barrier, len(plane) + len(column))

    def send(source, target, k, peer):
        pltpu.make_async_remote_copy(
            source, target, send_sem.at[k], recv_sem.at[k], device_id=peer, device_id_type=MESH
        ).start()

    def wait(buffer, count, semaphore):
        part = buffer.at[pl.ds(0, count)]
        pltpu.make_async_copy(part, part, semaphore).wait()

    for peer in plane:
        send(feat, plane_feat.at[here], 0, peer)
        send(place_row, plane_place.at[here], 1, peer)
    for peer in near:
        send(feat, near_feat.at[edge], 2, peer)
        send(place_row, near_place.at[edge], 3, peer)
    plane_feat[here] = feat[...]
    plane_place[here] = row
    near_feat[edge] = feat[...]
    near_place[edge] = row

    for copy in loads[2:]:
        copy.wait()
    own_feat = feat[...]
    cols = [
        dot(places, (iota((3, 128), 0) == k).astype(BF16), ((0,), (0,))) for k in range(3)
    ]
    own_norm = cols[0] * cols[0] + cols[1] * cols[1] + cols[2] * cols[2]
    dist = w_dist[...]
    base = 0.5 * (dot(own_feat, w_tgt[...]) + bias[...] + own_norm * dist)
    cross = [split2(-c * dist) for c in cols]
    dist_high, dist_mid = split2(jnp.broadcast_to(0.5 * dist, (16, 128)))
    base_high, base_mid = split2(base)
    stack = [c[0] for c in cross] + [c[1] for c in cross]
    stack += [dist_high] * 3 + [dist_mid] * 3 + [dist_high] * 3 + [base_high, base_mid]
    stack = jnp.concatenate(stack + [jnp.zeros((16, 128), BF16)] * (TERMS - len(stack)), axis=0)
    to, of = iota((512, 512), 0), iota((512, 512), 1)
    turned = dot((of == (to % TERMS) * 16 + to // TERMS).astype(BF16), stack).astype(BF16)
    src_half = w_src[...] * jnp.asarray(0.5, BF16)
    none = jnp.zeros((128, 128), BF16)
    for pair in range(8):
        wide[pair, :128, :128] = src_half
        wide[pair, :128, 128:] = src_half
        for side in range(2):
            at = (2 * pair + side) * TERMS
            wide[pair, 128 : 128 + TERMS, side * 128 : side * 128 + 128] = turned[at : at + TERMS]
        wide[pair, 128 + TERMS :, :] = jnp.zeros((128 - TERMS, 256), BF16)
    for full, part in ((edge_wide, w_edge), (coord_wide, w_coord)):
        halved = part[...] * jnp.asarray(0.5, BF16)
        full[:128, :128] = halved
        full[128:, 128:] = halved
        full[:128, 128:] = none
        full[128:, :128] = none

    mine = iota((16, 2048), 0) == iota((16, 2048), 1) // 128
    for pick, vector in ((gate_pick, 0.5 * w_gate[...]), (weight_pick, w_weight[...])):
        for side, part in enumerate(split2(vector)):
            part = jnp.concatenate([part.astype(F32)] * 16, axis=1)
            pick[side * 16 : side * 16 + 16, :] = jnp.where(mine, part, 0.0).astype(BF16)
    shared = (cols, wide, edge_wide[...], coord_wide[...], gate_pick, weight_pick, hidden, message, lifted)

    wait(near_feat, 7, recv_sem.at[2])
    wait(near_place, 7, recv_sem.at[3])
    for k in range(8):
        place_list[k : k + 1, :] = near_place[k]
    keep = (iota((16, 128), 1) != edge * 16 + iota((16, 128), 0)).astype(F32)
    near_rows = lambda at: near_feat[...].reshape(128, 128)
    message_own, coord_own = edge_sums(near_rows, place_list[0:8, :], 128, keep, *shared)

    wait(plane_feat, 31, recv_sem.at[0])
    wait(plane_place, 31, recv_sem.at[1])
    for side in range(2):
        for r in range(3):
            from_spot = table[r, here * 2 + side] // 2
            picked_feat[side, r] = plane_feat[from_spot]
            picked_place[side, r] = plane_place[from_spot]
    for peer, side in column:
        send(picked_feat.at[side], column_feat.at[spot], 4, peer)
        send(picked_place.at[side], column_place.at[spot], 5, peer)
    column_feat[spot] = picked_feat[z_hi]
    column_place[spot] = picked_place[z_hi]
    wait(column_feat, 15, recv_sem.at[4])
    wait(column_place, 15, recv_sem.at[5])
    for r in range(3):
        side = table[r, blk] % 2
        for k in range(8):
            at = r * 8 + k
            lhs[at * 16 : at * 16 + 16, :] = column_feat[side * 8 + k, r]
            place_list[at : at + 1, :] = column_place[side * 8 + k, r]
    far_rows = lambda at: lhs[at : at + 128, :]
    message_far, coord_far = edge_sums(far_rows, place_list[...], 384, None, *shared)

    mean_scale = 1.0 / 511
    mean = ((message_own + message_far) * mean_scale).astype(BF16)
    node_pre = dot(own_feat, w_in[:128, :]) + dot(mean, w_in[128:, :])
    node_hidden = (node_pre * jax.nn.sigmoid(node_pre)).astype(BF16)
    feat_out[...] = (own_feat.astype(F32) + dot(node_hidden, w_out[...])).astype(BF16)
    eye = iota((16, 16), 0) == iota((16, 16), 1)
    for k in range(3):
        moved = jnp.sum(jnp.where(eye, coord_own[k] + coord_far[k], 0.0), axis=0, keepdims=True)
        place_out[k : k + 1, :] = places[k : k + 1].astype(F32) + mean_scale * moved

    for k, buffer, count in (
        (0, plane_feat, 31), (1, plane_place, 31), (2, near_feat, 7), (3, near_place, 7),
        (4, column_feat, 15), (5, column_place, 15),
    ):
        wait(buffer, count, send_sem.at[k])


def shards(*args):
    args = [a.reshape(1, -1) if a.ndim == 1 else a for a in args]
    vmem = lambda shape, kind: pltpu.VMEM(shape, kind)
    loaded = [
        pltpu.SMEM(a.shape, a.dtype) if a.dtype == jnp.int32 else pltpu.VMEM(a.shape, a.dtype) for a in args
    ]
    return pl.pallas_call(
        layer,
        out_shape=(jax.ShapeDtypeStruct((ROWS, 128), BF16), jax.ShapeDtypeStruct((3, ROWS), F32)),
        in_specs=[pl.BlockSpec(memory_space=pltpu.HBM)] * len(args),
        out_specs=(pl.BlockSpec(memory_space=pltpu.VMEM), pl.BlockSpec(memory_space=pltpu.VMEM)),
        scratch_shapes=loaded
        + [
            vmem((1, 128), F32),
            vmem((8, 16, 128), BF16),
            vmem((8, 1, 128), F32),
            vmem((32, 16, 128), BF16),
            vmem((32, 1, 128), F32),
            vmem((2, 3, 16, 128), BF16),
            vmem((2, 3, 1, 128), F32),
            vmem((16, 3, 16, 128), BF16),
            vmem((16, 3, 1, 128), F32),
            vmem((384, 128), BF16),
            vmem((24, 128), F32),
            vmem((8, 256, 256), BF16),
            vmem((256, 256), BF16),
            vmem((256, 256), BF16),
            vmem((32, 2048), BF16),
            vmem((32, 2048), BF16),
            vmem((384, 2048), BF16),
            vmem((384, 2048), BF16),
            vmem((384, 2048), BF16),
            pltpu.SemaphoreType.DMA((13,)),
            pltpu.SemaphoreType.DMA((6,)),
            pltpu.SemaphoreType.DMA((6,)),
        ],
        compiler_params=pltpu.CompilerParams(
            collective_id=0, has_side_effects=True, vmem_limit_bytes=60 * 1024 * 1024
        ),
    )(*args)


def solution(mesh):
    specs = (P(("blk", "edge"), None), P(None, ("blk", "edge"))) + (P(),) * 11
    return jax.shard_map(
        shards,
        mesh=mesh,
        in_specs=specs,
        out_specs=(P(("blk", "edge"), None), P(None, ("blk", "edge"))),
        check_vma=False,
    )
```

```python
import functools

import jax
import jax.numpy as jnp
from jax import lax
from jax.experimental import pallas as pl
from jax.experimental.pallas import tpu as pltpu
from jax.sharding import PartitionSpec as P

MESH = pl.DeviceIdType.MESH
F32 = jnp.float32
BF16 = jnp.bfloat16

NX, NY, NZ = 4, 8, 8
RING = {4: (2, 1, 3, 0), 8: (4, 3, 5, 2, 6, 1, 7, 0)}
PLANE = [(dx, dy) for dx in RING[NX] for dy in RING[NY] if dx or dy]
COLUMN = [(dz, dc) for dz in RING[NZ] for dc in (1, 0) if dz or dc]
EDGE = (4, 3, 5, 2, 6, 1, 7)
ROWS = 16
TERMS = 32


def iota(shape, dim):
    return lax.broadcasted_iota(jnp.int32, shape, dim)


def dot(a, b, dims=((1,), (0,))):
    return lax.dot_general(a, b, (dims, ((), ())), preferred_element_type=F32)


def split2(a):
    high = a.astype(BF16)
    return high, (a - high.astype(F32)).astype(BF16)


def half_silu(h):
    return h + h * jnp.tanh(h)


def place_terms(places, count):
    slots = places.shape[0]
    spread = jnp.broadcast_to(places[:, None, :], (slots, 16, 128)).reshape(count, 128)
    lane, node = iota((count, 128), 1), lax.rem(iota((count, 128), 0), 16)
    spread = jnp.where(lax.rem(lane, 16) == node, spread, 0.0)
    square_high, square_low = split2(spread * spread)
    parts = jnp.concatenate([spread.astype(BF16), square_high, square_low], axis=1)
    row, term = iota((384, 128), 0), iota((384, 128), 1)
    axis = lax.rem(row, 128) // 16
    kind = row // 128
    first = jnp.where(kind == 0, 0, 6 * kind)
    hit = (term == first + axis) | ((kind < 2) & (term == first + 3 + axis))
    placed = dot(parts, ((axis < 3) & hit).astype(BF16))
    ones = (lane == 15) | (lane == 16)
    return jnp.where(ones, 1.0, placed).astype(BF16)


def edge_sums(feats, places, count, own, target_cols, wide, w_edge2, w_coord2, gate_pick, weight_pick, hidden, message, lifted):
    terms = place_terms(places, count)
    chunks = [(at, pair) for pair in range(8) for at in range(0, count, 128)]
    lhs = [jnp.concatenate([feats(at), terms[at : at + 128]], axis=1) for at in range(0, count, 128)]
    for at, pair in chunks:
        half = dot(lhs[at // 128], wide[pair]).astype(BF16)
        hidden[at : at + 128, pair * 256 : pair * 256 + 256] = half_silu(half)

    rows8 = dot((iota((8, 128), 0) == iota((8, 128), 1)).astype(BF16), terms, ((1,), (1,)))
    offsets = [target_cols[k][:, :1] - rows8[k : k + 1] for k in range(3)]
    radial = offsets[0] * offsets[0] + offsets[1] * offsets[1] + offsets[2] * offsets[2]
    scale = 1.0 / (jnp.sqrt(radial) + 1.0)

    for at, pair in chunks:
        half = dot(hidden[at : at + 128, pair * 256 : pair * 256 + 256], w_edge2).astype(BF16)
        message[at : at + 128, pair * 256 : pair * 256 + 256] = half_silu(half)
    for at, pair in chunks:
        half = dot(message[at : at + 128, pair * 256 : pair * 256 + 256], w_coord2).astype(BF16)
        lifted[at : at + 128, pair * 256 : pair * 256 + 256] = half_silu(half)
    messages = message[:count, :]
    logit = dot(gate_pick[...], messages, ((1,), (1,)))
    gate = 0.5 + 0.5 * jnp.tanh(logit[:16] + logit[16:])
    weight = dot(weight_pick[...], lifted[:count, :], ((1,), (1,)))
    weight = (weight[:16] + weight[16:]) * scale
    if own is not None:
        gate, weight = gate * own, weight * own
    spread = dot(gate.astype(BF16), messages)
    row = iota((16, 128), 0)
    message_sum = jnp.zeros((16, 128), F32)
    for i in range(16):
        message_sum = message_sum + jnp.where(row == i, spread[:, i * 128 : i * 128 + 128], 0.0)
    coord_sum = [jnp.sum(offsets[k] * weight, axis=1, keepdims=True) for k in range(3)]
    return message_sum, coord_sum


def layer(
    feat_hbm, place_hbm, table_hbm, w_tgt_hbm, w_src_hbm, w_dist_hbm, bias_hbm, w_edge_hbm, w_gate_hbm,
    w_coord_hbm, w_weight_hbm, w_in_hbm, w_out_hbm,
    feat_out, place_out,
    feat, place, table, w_tgt, w_src, w_dist, bias, w_edge, w_gate, w_coord, w_weight, w_in, w_out,
    place_row, near_feat, near_place, plane_feat, plane_place, picked_feat, picked_place,
    column_feat, column_place, lhs, place_list, wide, edge_wide, coord_wide, gate_pick, weight_pick,
    hidden, message, lifted,
    load_sem, send_sem, recv_sem,
):
    blk, edge = lax.axis_index("blk"), lax.axis_index("edge")
    x, y, z_hi = blk // 16, (blk // 2) % 8, blk % 2
    core = edge % 2
    z = z_hi * 4 + edge // 2
    here = x * 8 + y
    spot = z * 2 + core

    plane = [{"blk": (lax.rem(x + dx, NX) * NY + lax.rem(y + dy, NY)) * 2 + z_hi} for dx, dy in PLANE]
    column = []
    for dz, dc in COLUMN:
        z_to = lax.rem(z + dz, NZ)
        column.append(({"blk": here * 2 + z_to // 4, "edge": (z_to % 4) * 2 + lax.rem(core + dc, 2)}, z_to // 4))
    near = [{"edge": lax.rem(edge + step, 8)} for step in EDGE]

    barrier = pltpu.get_barrier_semaphore()
    for peer in plane + [c[0] for c in column]:
        pl.semaphore_signal(barrier, inc=1, device_id=peer, device_id_type=MESH)
    loads = [
        pltpu.make_async_copy(a, b, load_sem.at[k])
        for k, (a, b) in enumerate(
            [
                (feat_hbm, feat), (place_hbm, place), (table_hbm, table), (w_tgt_hbm, w_tgt), (w_src_hbm, w_src),
                (w_dist_hbm, w_dist), (bias_hbm, bias), (w_edge_hbm, w_edge), (w_gate_hbm, w_gate),
                (w_coord_hbm, w_coord), (w_weight_hbm, w_weight), (w_in_hbm, w_in), (w_out_hbm, w_out),
            ]
        )
    ]
    for copy in loads:
        copy.start()
    loads[0].wait()
    loads[1].wait()
    places = place[...]
    row = jnp.zeros((1, 128), F32)
    for k in range(3):
        row = row + dot(places[k : k + 1], (iota((16, 128), 0) + 16 * k == iota((16, 128), 1)).astype(BF16))
    place_row[...] = row
    pl.semaphore_wait(barrier, len(plane) + len(column))

    def send(source, target, k, peer):
        pltpu.make_async_remote_copy(
            source, target, send_sem.at[k], recv_sem.at[k], device_id=peer, device_id_type=MESH
        ).start()

    def wait(buffer, count, semaphore):
        part = buffer.at[pl.ds(0, count)]
        pltpu.make_async_copy(part, part, semaphore).wait()

    for peer in plane:
        send(feat, plane_feat.at[here], 0, peer)
        send(place_row, plane_place.at[here], 1, peer)
    for peer in near:
        send(feat, near_feat.at[edge], 2, peer)
        send(place_row, near_place.at[edge], 3, peer)
    plane_feat[here] = feat[...]
    plane_place[here] = row
    near_feat[edge] = feat[...]
    near_place[edge] = row

    for copy in loads[2:]:
        copy.wait()
    own_feat = feat[...]
    cols = [
        dot(places, (iota((3, 128), 0) == k).astype(BF16), ((0,), (0,))) for k in range(3)
    ]
    own_norm = cols[0] * cols[0] + cols[1] * cols[1] + cols[2] * cols[2]
    dist = w_dist[...]
    base = 0.5 * (dot(own_feat, w_tgt[...]) + bias[...] + own_norm * dist)
    cross = [split2(-c * dist) for c in cols]
    dist_high, dist_mid = split2(jnp.broadcast_to(0.5 * dist, (16, 128)))
    base_high, base_mid = split2(base)
    stack = [c[0] for c in cross] + [c[1] for c in cross]
    stack += [dist_high] * 3 + [dist_mid] * 3 + [dist_high] * 3 + [base_high, base_mid]
    stack = jnp.concatenate(stack + [jnp.zeros((16, 128), BF16)] * (TERMS - len(stack)), axis=0)
    to, of = iota((512, 512), 0), iota((512, 512), 1)
    turned = dot((of == (to % TERMS) * 16 + to // TERMS).astype(BF16), stack).astype(BF16)
    src_half = w_src[...] * jnp.asarray(0.5, BF16)
    none = jnp.zeros((128, 128), BF16)
    for pair in range(8):
        wide[pair, :128, :128] = src_half
        wide[pair, :128, 128:] = src_half
        for side in range(2):
            at = (2 * pair + side) * TERMS
            wide[pair, 128 : 128 + TERMS, side * 128 : side * 128 + 128] = turned[at : at + TERMS]
        wide[pair, 128 + TERMS :, :] = jnp.zeros((128 - TERMS, 256), BF16)
    for full, part in ((edge_wide, w_edge), (coord_wide, w_coord)):
        halved = part[...] * jnp.asarray(0.5, BF16)
        full[:128, :128] = halved
        full[128:, 128:] = halved
        full[:128, 128:] = none
        full[128:, :128] = none

    mine = iota((16, 2048), 0) == iota((16, 2048), 1) // 128
    for pick, vector in ((gate_pick, 0.5 * w_gate[...]), (weight_pick, w_weight[...])):
        for side, part in enumerate(split2(vector)):
            part = jnp.concatenate([part.astype(F32)] * 16, axis=1)
            pick[side * 16 : side * 16 + 16, :] = jnp.where(mine, part, 0.0).astype(BF16)
    shared = (cols, wide, edge_wide[...], coord_wide[...], gate_pick, weight_pick, hidden, message, lifted)

    wait(plane_feat, 31, recv_sem.at[0])
    wait(plane_place, 31, recv_sem.at[1])
    for side in range(2):
        for r in range(3):
            from_spot = table[r, here * 2 + side] // 2
            picked_feat[side, r] = plane_feat[from_spot]
            picked_place[side, r] = plane_place[from_spot]
    for z_to in range(NZ):
      for c_to in range(2):
        @pl.when(spot != z_to * 2 + c_to)
        def _(z_to=z_to, c_to=c_to):
            peer = {"blk": here * 2 + z_to // 4, "edge": (z_to % 4) * 2 + c_to}
            send(picked_feat.at[z_to // 4], column_feat.at[spot], 4, peer)
            send(picked_place.at[z_to // 4], column_place.at[spot], 5, peer)
    column_feat[spot] = picked_feat[z_hi]
    column_place[spot] = picked_place[z_hi]
    wait(near_feat, 7, recv_sem.at[2])
    wait(near_place, 7, recv_sem.at[3])
    for k in range(8):
        place_list[k : k + 1, :] = near_place[k]
    keep = (iota((16, 128), 1) != edge * 16 + iota((16, 128), 0)).astype(F32)
    near_rows = lambda at: near_feat[...].reshape(128, 128)
    message_own, coord_own = edge_sums(near_rows, place_list[0:8, :], 128, keep, *shared)

    wait(column_feat, 15, recv_sem.at[4])
    wait(column_place, 15, recv_sem.at[5])
    for r in range(3):
        side = table[r, blk] % 2
        for k in range(8):
            at = r * 8 + k
            lhs[at * 16 : at * 16 + 16, :] = column_feat[side * 8 + k, r]
            place_list[at : at + 1, :] = column_place[side * 8 + k, r]
    far_rows = lambda at: lhs[at : at + 128, :]
    message_far, coord_far = edge_sums(far_rows, place_list[...], 384, None, *shared)

    mean_scale = 1.0 / 511
    mean = ((message_own + message_far) * mean_scale).astype(BF16)
    node_pre = dot(own_feat, w_in[:128, :]) + dot(mean, w_in[128:, :])
    node_hidden = (node_pre * jax.nn.sigmoid(node_pre)).astype(BF16)
    feat_out[...] = (own_feat.astype(F32) + dot(node_hidden, w_out[...])).astype(BF16)
    eye = iota((16, 16), 0) == iota((16, 16), 1)
    for k in range(3):
        moved = jnp.sum(jnp.where(eye, coord_own[k] + coord_far[k], 0.0), axis=0, keepdims=True)
        place_out[k : k + 1, :] = places[k : k + 1].astype(F32) + mean_scale * moved

    for k, buffer, count in (
        (0, plane_feat, 31), (1, plane_place, 31), (2, near_feat, 7), (3, near_place, 7),
        (4, column_feat, 15), (5, column_place, 15),
    ):
        wait(buffer, count, send_sem.at[k])


def shards(*args):
    args = [a.reshape(1, -1) if a.ndim == 1 else a for a in args]
    vmem = lambda shape, kind: pltpu.VMEM(shape, kind)
    loaded = [
        pltpu.SMEM(a.shape, a.dtype) if a.dtype == jnp.int32 else pltpu.VMEM(a.shape, a.dtype) for a in args
    ]
    args = [pltpu.with_memory_space_constraint(a, pltpu.HBM) for a in args]
    return pl.pallas_call(
        layer,
        out_shape=(pltpu.VMEM((ROWS, 128), BF16), pltpu.VMEM((3, ROWS), F32)),
        in_specs=[pl.BlockSpec(memory_space=pltpu.HBM)] * len(args),
        out_specs=(pl.BlockSpec(memory_space=pltpu.VMEM), pl.BlockSpec(memory_space=pltpu.VMEM)),
        scratch_shapes=loaded
        + [
            vmem((1, 128), F32),
            vmem((8, 16, 128), BF16),
            vmem((8, 1, 128), F32),
            vmem((32, 16, 128), BF16),
            vmem((32, 1, 128), F32),
            vmem((2, 3, 16, 128), BF16),
            vmem((2, 3, 1, 128), F32),
            vmem((16, 3, 16, 128), BF16),
            vmem((16, 3, 1, 128), F32),
            vmem((384, 128), BF16),
            vmem((24, 128), F32),
            vmem((8, 256, 256), BF16),
            vmem((256, 256), BF16),
            vmem((256, 256), BF16),
            vmem((32, 2048), BF16),
            vmem((32, 2048), BF16),
            vmem((384, 2048), BF16),
            vmem((384, 2048), BF16),
            vmem((384, 2048), BF16),
            pltpu.SemaphoreType.DMA((13,)),
            pltpu.SemaphoreType.DMA((6,)),
            pltpu.SemaphoreType.DMA((6,)),
        ],
        compiler_params=pltpu.CompilerParams(
            collective_id=0, has_side_effects=True, vmem_limit_bytes=40 * 1024 * 1024
        ),
    )(*args)


def solution(mesh):
    specs = (P(("blk", "edge"), None), P(None, ("blk", "edge"))) + (P(),) * 11
    return jax.shard_map(
        shards,
        mesh=mesh,
        in_specs=specs,
        out_specs=(P(("blk", "edge"), None), P(None, ("blk", "edge"))),
        check_vma=False,
    )
```

```python
import functools

import jax
import jax.numpy as jnp
from jax import lax
from jax.experimental import pallas as pl
from jax.experimental.pallas import tpu as pltpu
from jax.sharding import PartitionSpec as P

MESH = pl.DeviceIdType.MESH
F32 = jnp.float32
BF16 = jnp.bfloat16

NX, NY, NZ = 4, 8, 8
RING = {4: (2, 1, 3, 0), 8: (4, 3, 5, 2, 6, 1, 7, 0)}
PLANE = [(dx, dy) for dx in RING[NX] for dy in RING[NY] if dx or dy]
COLUMN = [(dz, dc) for dz in RING[NZ] for dc in (1, 0) if dz or dc]
EDGE = (4, 3, 5, 2, 6, 1, 7)
ROWS = 16
TERMS = 32


def iota(shape, dim):
    return lax.broadcasted_iota(jnp.int32, shape, dim)


def dot(a, b, dims=((1,), (0,))):
    return lax.dot_general(a, b, (dims, ((), ())), preferred_element_type=F32)


def split2(a):
    high = a.astype(BF16)
    return high, (a - high.astype(F32)).astype(BF16)


def half_silu(h):
    return h + h * jnp.tanh(h)


def place_terms(places, count):
    slots = places.shape[0]
    spread = jnp.broadcast_to(places[:, None, :], (slots, 16, 128)).reshape(count, 128)
    lane, node = iota((count, 128), 1), lax.rem(iota((count, 128), 0), 16)
    spread = jnp.where(lax.rem(lane, 16) == node, spread, 0.0)
    square_high, square_low = split2(spread * spread)
    parts = jnp.concatenate([spread.astype(BF16), square_high, square_low], axis=1)
    row, term = iota((384, 128), 0), iota((384, 128), 1)
    axis = lax.rem(row, 128) // 16
    kind = row // 128
    first = jnp.where(kind == 0, 0, 6 * kind)
    hit = (term == first + axis) | ((kind < 2) & (term == first + 3 + axis))
    placed = dot(parts, ((axis < 3) & hit).astype(BF16))
    ones = (lane == 15) | (lane == 16)
    return jnp.where(ones, 1.0, placed).astype(BF16)


def edge_sums(feats, places, count, own, target_cols, wide, w_edge2, w_coord2, gate_pick, weight_pick, hidden, message, lifted):
    terms = place_terms(places, count)
    chunks = [(at, pair) for pair in range(8) for at in range(0, count, 128)]
    lhs = [jnp.concatenate([feats(at), terms[at : at + 128]], axis=1) for at in range(0, count, 128)]
    for at, pair in chunks:
        half = dot(lhs[at // 128], wide[pair]).astype(BF16)
        hidden[at : at + 128, pair * 256 : pair * 256 + 256] = half_silu(half)

    rows8 = dot((iota((8, 128), 0) == iota((8, 128), 1)).astype(BF16), terms, ((1,), (1,)))
    offsets = [target_cols[k][:, :1] - rows8[k : k + 1] for k in range(3)]
    radial = offsets[0] * offsets[0] + offsets[1] * offsets[1] + offsets[2] * offsets[2]
    scale = 1.0 / (jnp.sqrt(radial) + 1.0)

    for at, pair in chunks:
        half = dot(hidden[at : at + 128, pair * 256 : pair * 256 + 256], w_edge2).astype(BF16)
        message[at : at + 128, pair * 256 : pair * 256 + 256] = half_silu(half)
    for at, pair in chunks:
        half = dot(message[at : at + 128, pair * 256 : pair * 256 + 256], w_coord2).astype(BF16)
        lifted[at : at + 128, pair * 256 : pair * 256 + 256] = half_silu(half)
    messages = message[:count, :]
    logit = dot(gate_pick[...], messages, ((1,), (1,)))
    gate = 0.5 + 0.5 * jnp.tanh(logit[:16] + logit[16:])
    weight = dot(weight_pick[...], lifted[:count, :], ((1,), (1,)))
    weight = (weight[:16] + weight[16:]) * scale
    if own is not None:
        gate, weight = gate * own, weight * own
    spread = dot(gate.astype(BF16), messages)
    row = iota((16, 128), 0)
    message_sum = jnp.zeros((16, 128), F32)
    for i in range(16):
        message_sum = message_sum + jnp.where(row == i, spread[:, i * 128 : i * 128 + 128], 0.0)
    coord_sum = [jnp.sum(offsets[k] * weight, axis=1, keepdims=True) for k in range(3)]
    return message_sum, coord_sum


def layer(
    feat_hbm, place_hbm, table_hbm, w_tgt_hbm, w_src_hbm, w_dist_hbm, bias_hbm, w_edge_hbm, w_gate_hbm,
    w_coord_hbm, w_weight_hbm, w_in_hbm, w_out_hbm,
    feat_out, place_out,
    feat, place, table, w_tgt, w_src, w_dist, bias, w_edge, w_gate, w_coord, w_weight, w_in, w_out,
    place_row, near_feat, near_place, plane_feat, plane_place, picked_feat, picked_place,
    column_feat, column_place, lhs, place_list, wide, edge_wide, coord_wide, gate_pick, weight_pick,
    hidden, message, lifted,
    load_sem, send_sem, recv_sem,
):
    blk, edge = lax.axis_index("blk"), lax.axis_index("edge")
    x, y, z_hi = blk // 16, (blk // 2) % 8, blk % 2
    core = edge % 2
    z = z_hi * 4 + edge // 2
    here = x * 8 + y
    spot = z * 2 + core

    plane = [{"blk": (lax.rem(x + dx, NX) * NY + lax.rem(y + dy, NY)) * 2 + z_hi} for dx, dy in PLANE]
    column = []
    for dz, dc in COLUMN:
        z_to = lax.rem(z + dz, NZ)
        column.append(({"blk": here * 2 + z_to // 4, "edge": (z_to % 4) * 2 + lax.rem(core + dc, 2)}, z_to // 4))
    near = [{"edge": lax.rem(edge + step, 8)} for step in EDGE]

    barrier = pltpu.get_barrier_semaphore()
    for peer in plane + [c[0] for c in column]:
        pl.semaphore_signal(barrier, inc=1, device_id=peer, device_id_type=MESH)
    loads = [
        pltpu.make_async_copy(a, b, load_sem.at[k])
        for k, (a, b) in enumerate(
            [
                (feat_hbm, feat), (place_hbm, place), (table_hbm, table), (w_tgt_hbm, w_tgt), (w_src_hbm, w_src),
                (w_dist_hbm, w_dist), (bias_hbm, bias), (w_edge_hbm, w_edge), (w_gate_hbm, w_gate),
                (w_coord_hbm, w_coord), (w_weight_hbm, w_weight), (w_in_hbm, w_in), (w_out_hbm, w_out),
            ]
        )
    ]
    for copy in loads:
        copy.start()
    loads[0].wait()
    loads[1].wait()
    places = place[...]
    row = jnp.zeros((1, 128), F32)
    for k in range(3):
        row = row + dot(places[k : k + 1], (iota((16, 128), 0) + 16 * k == iota((16, 128), 1)).astype(BF16))
    place_row[...] = row
    pl.semaphore_wait(barrier, len(plane) + len(column))

    def send(source, target, k, peer):
        pltpu.make_async_remote_copy(
            source, target, send_sem.at[k], recv_sem.at[k], device_id=peer, device_id_type=MESH
        ).start()

    def wait(buffer, count, semaphore):
        part = buffer.at[pl.ds(0, count)]
        pltpu.make_async_copy(part, part, semaphore).wait()

    for peer in plane:
        send(feat, plane_feat.at[here], 0, peer)
        send(place_row, plane_place.at[here], 1, peer)
    for peer in near:
        send(feat, near_feat.at[edge], 2, peer)
        send(place_row, near_place.at[edge], 3, peer)
    plane_feat[here] = feat[...]
    plane_place[here] = row
    near_feat[edge] = feat[...]
    near_place[edge] = row

    for copy in loads[2:]:
        copy.wait()
    own_feat = feat[...]
    cols = [
        dot(places, (iota((3, 128), 0) == k).astype(BF16), ((0,), (0,))) for k in range(3)
    ]
    own_norm = cols[0] * cols[0] + cols[1] * cols[1] + cols[2] * cols[2]
    dist = w_dist[...]
    base = 0.5 * (dot(own_feat, w_tgt[...]) + bias[...] + own_norm * dist)
    cross = [split2(-c * dist) for c in cols]
    dist_high, dist_mid = split2(jnp.broadcast_to(0.5 * dist, (16, 128)))
    base_high, base_mid = split2(base)
    stack = [c[0] for c in cross] + [c[1] for c in cross]
    stack += [dist_high] * 3 + [dist_mid] * 3 + [dist_high] * 3 + [base_high, base_mid]
    stack = jnp.concatenate(stack + [jnp.zeros((16, 128), BF16)] * (TERMS - len(stack)), axis=0)
    to, of = iota((512, 512), 0), iota((512, 512), 1)
    turned = dot((of == (to % TERMS) * 16 + to // TERMS).astype(BF16), stack).astype(BF16)
    src_half = w_src[...] * jnp.asarray(0.5, BF16)
    none = jnp.zeros((128, 128), BF16)
    for pair in range(8):
        wide[pair, :128, :128] = src_half
        wide[pair, :128, 128:] = src_half
        for side in range(2):
            at = (2 * pair + side) * TERMS
            wide[pair, 128 : 128 + TERMS, side * 128 : side * 128 + 128] = turned[at : at + TERMS]
        wide[pair, 128 + TERMS :, :] = jnp.zeros((128 - TERMS, 256), BF16)
    for full, part in ((edge_wide, w_edge), (coord_wide, w_coord)):
        halved = part[...] * jnp.asarray(0.5, BF16)
        full[:128, :128] = halved
        full[128:, 128:] = halved
        full[:128, 128:] = none
        full[128:, :128] = none

    mine = iota((16, 2048), 0) == iota((16, 2048), 1) // 128
    for pick, vector in ((gate_pick, 0.5 * w_gate[...]), (weight_pick, w_weight[...])):
        for side, part in enumerate(split2(vector)):
            part = jnp.concatenate([part.astype(F32)] * 16, axis=1)
            pick[side * 16 : side * 16 + 16, :] = jnp.where(mine, part, 0.0).astype(BF16)
    shared = (cols, wide, edge_wide[...], coord_wide[...], gate_pick, weight_pick, hidden, message, lifted)

    wait(plane_feat, 31, recv_sem.at[0])
    wait(plane_place, 31, recv_sem.at[1])
    for side in range(2):
        for r in range(3):
            from_spot = table[r, here * 2 + side] // 2
            picked_feat[side, r] = plane_feat[from_spot]
            picked_place[side, r] = plane_place[from_spot]
    for z_to in range(NZ):
      for c_to in range(2):
        @pl.when(spot != z_to * 2 + c_to)
        def _(z_to=z_to, c_to=c_to):
            peer = {"blk": here * 2 + z_to // 4, "edge": (z_to % 4) * 2 + c_to}
            send(picked_feat.at[z_to // 4], column_feat.at[spot], 4, peer)
            send(picked_place.at[z_to // 4], column_place.at[spot], 5, peer)
    column_feat[spot] = picked_feat[z_hi]
    column_place[spot] = picked_place[z_hi]
    wait(near_feat, 7, recv_sem.at[2])
    wait(near_place, 7, recv_sem.at[3])
    for k in range(8):
        place_list[k : k + 1, :] = near_place[k]
    keep = (iota((16, 128), 1) != edge * 16 + iota((16, 128), 0)).astype(F32)
    near_rows = lambda at: near_feat[...].reshape(128, 128)
    message_own, coord_own = edge_sums(near_rows, place_list[0:8, :], 128, keep, *shared)

    wait(column_feat, 15, recv_sem.at[4])
    wait(column_place, 15, recv_sem.at[5])
    for r in range(3):
        side = table[r, blk] % 2
        for k in range(8):
            at = r * 8 + k
            lhs[at * 16 : at * 16 + 16, :] = column_feat[side * 8 + k, r]
            place_list[at : at + 1, :] = column_place[side * 8 + k, r]
    far_rows = lambda at: lhs[at : at + 128, :]
    message_far, coord_far = edge_sums(far_rows, place_list[...], 384, None, *shared)

    mean_scale = 1.0 / 511
    mean = ((message_own + message_far) * mean_scale).astype(BF16)
    node_pre = dot(own_feat, w_in[:128, :]) + dot(mean, w_in[128:, :])
    node_hidden = (node_pre * jax.nn.sigmoid(node_pre)).astype(BF16)
    feat_out[...] = (own_feat.astype(F32) + dot(node_hidden, w_out[...])).astype(BF16)
    eye = iota((16, 16), 0) == iota((16, 16), 1)
    for k in range(3):
        moved = jnp.sum(jnp.where(eye, coord_own[k] + coord_far[k], 0.0), axis=0, keepdims=True)
        place_out[k : k + 1, :] = places[k : k + 1].astype(F32) + mean_scale * moved

    for k, buffer, count in (
        (0, plane_feat, 31), (1, plane_place, 31), (2, near_feat, 7), (3, near_place, 7),
        (4, column_feat, 15), (5, column_place, 15),
    ):
        wait(buffer, count, send_sem.at[k])


def deliver(feat_in, place_in, feat_out, place_out, sems):
    copies = [
        pltpu.make_async_copy(feat_in, feat_out, sems.at[0]),
        pltpu.make_async_copy(place_in, place_out, sems.at[1]),
    ]
    for copy in copies:
        copy.start()
    for copy in copies:
        copy.wait()


def shards(*args):
    args = [a.reshape(1, -1) if a.ndim == 1 else a for a in args]
    vmem = lambda shape, kind: pltpu.VMEM(shape, kind)
    loaded = [
        pltpu.SMEM(a.shape, a.dtype) if a.dtype == jnp.int32 else pltpu.VMEM(a.shape, a.dtype) for a in args
    ]
    args = [pltpu.with_memory_space_constraint(a, pltpu.HBM) for a in args]
    results = pl.pallas_call(
        layer,
        out_shape=(pltpu.VMEM((ROWS, 128), BF16), pltpu.VMEM((3, ROWS), F32)),
        in_specs=[pl.BlockSpec(memory_space=pltpu.HBM)] * len(args),
        out_specs=(pl.BlockSpec(memory_space=pltpu.VMEM), pl.BlockSpec(memory_space=pltpu.VMEM)),
        scratch_shapes=loaded
        + [
            vmem((1, 128), F32),
            vmem((8, 16, 128), BF16),
            vmem((8, 1, 128), F32),
            vmem((32, 16, 128), BF16),
            vmem((32, 1, 128), F32),
            vmem((2, 3, 16, 128), BF16),
            vmem((2, 3, 1, 128), F32),
            vmem((16, 3, 16, 128), BF16),
            vmem((16, 3, 1, 128), F32),
            vmem((384, 128), BF16),
            vmem((24, 128), F32),
            vmem((8, 256, 256), BF16),
            vmem((256, 256), BF16),
            vmem((256, 256), BF16),
            vmem((32, 2048), BF16),
            vmem((32, 2048), BF16),
            vmem((384, 2048), BF16),
            vmem((384, 2048), BF16),
            vmem((384, 2048), BF16),
            pltpu.SemaphoreType.DMA((13,)),
            pltpu.SemaphoreType.DMA((6,)),
            pltpu.SemaphoreType.DMA((6,)),
        ],
        compiler_params=pltpu.CompilerParams(
            collective_id=0, has_side_effects=True, vmem_limit_bytes=40 * 1024 * 1024
        ),
    )(*args)
    return pl.pallas_call(
        deliver,
        out_shape=(jax.ShapeDtypeStruct((ROWS, 128), BF16), jax.ShapeDtypeStruct((3, ROWS), F32)),
        in_specs=[pl.BlockSpec(memory_space=pltpu.VMEM)] * 2,
        out_specs=(pl.BlockSpec(memory_space=pltpu.HBM),) * 2,
        scratch_shapes=[pltpu.SemaphoreType.DMA((2,))],
    )(*[pltpu.with_memory_space_constraint(r, pltpu.VMEM) for r in results])


def solution(mesh):
    specs = (P(("blk", "edge"), None), P(None, ("blk", "edge"))) + (P(),) * 11
    return jax.shard_map(
        shards,
        mesh=mesh,
        in_specs=specs,
        out_specs=(P(("blk", "edge"), None), P(None, ("blk", "edge"))),
        check_vma=False,
    )
```

```python
import functools

import jax
import jax.numpy as jnp
from jax import lax
from jax.experimental import pallas as pl
from jax.experimental.pallas import tpu as pltpu
from jax.sharding import PartitionSpec as P

MESH = pl.DeviceIdType.MESH
F32 = jnp.float32
BF16 = jnp.bfloat16

NX, NY, NZ = 4, 8, 8
RING = {4: (2, 1, 3, 0), 8: (4, 3, 5, 2, 6, 1, 7, 0)}
PLANE = [(dx, dy) for dx in RING[NX] for dy in RING[NY] if dx or dy]
EDGE = (4, 3, 5, 2, 6, 1, 7)
ROWS = 16
TERMS = 32


def iota(shape, dim):
    return lax.broadcasted_iota(jnp.int32, shape, dim)


def dot(a, b, dims=((1,), (0,))):
    return lax.dot_general(a, b, (dims, ((), ())), preferred_element_type=F32)


def split2(a):
    high = a.astype(BF16)
    return high, (a - high.astype(F32)).astype(BF16)


def half_silu(h):
    return h + h * jnp.tanh(h)


def place_terms(places, count):
    slots = places.shape[0]
    spread = jnp.broadcast_to(places[:, None, :], (slots, 16, 128)).reshape(count, 128)
    lane, node = iota((count, 128), 1), lax.rem(iota((count, 128), 0), 16)
    spread = jnp.where(lax.rem(lane, 16) == node, spread, 0.0)
    square_high, square_low = split2(spread * spread)
    parts = jnp.concatenate([spread.astype(BF16), square_high, square_low], axis=1)
    row, term = iota((384, 128), 0), iota((384, 128), 1)
    axis = lax.rem(row, 128) // 16
    kind = row // 128
    first = jnp.where(kind == 0, 0, 6 * kind)
    hit = (term == first + axis) | ((kind < 2) & (term == first + 3 + axis))
    placed = dot(parts, ((axis < 3) & hit).astype(BF16))
    ones = (lane == 15) | (lane == 16)
    return jnp.where(ones, 1.0, placed).astype(BF16)


def edge_sums(feats, places, count, own, target_cols, wide, w_edge2, w_coord2, gate_pick, weight_pick, hidden, message, lifted):
    terms = place_terms(places, count)
    chunks = [(at, pair) for pair in range(8) for at in range(0, count, 128)]
    lhs = [jnp.concatenate([feats(at), terms[at : at + 128]], axis=1) for at in range(0, count, 128)]
    for at, pair in chunks:
        half = dot(lhs[at // 128], wide[pair]).astype(BF16)
        hidden[at : at + 128, pair * 256 : pair * 256 + 256] = half_silu(half)

    rows8 = dot((iota((8, 128), 0) == iota((8, 128), 1)).astype(BF16), terms, ((1,), (1,)))
    offsets = [target_cols[k][:, :1] - rows8[k : k + 1] for k in range(3)]
    radial = offsets[0] * offsets[0] + offsets[1] * offsets[1] + offsets[2] * offsets[2]
    scale = 1.0 / (jnp.sqrt(radial) + 1.0)

    for at, pair in chunks:
        half = dot(hidden[at : at + 128, pair * 256 : pair * 256 + 256], w_edge2).astype(BF16)
        message[at : at + 128, pair * 256 : pair * 256 + 256] = half_silu(half)
    for at, pair in chunks:
        half = dot(message[at : at + 128, pair * 256 : pair * 256 + 256], w_coord2).astype(BF16)
        lifted[at : at + 128, pair * 256 : pair * 256 + 256] = half_silu(half)
    messages = message[:count, :]
    logit = dot(gate_pick[...], messages, ((1,), (1,)))
    gate = 0.5 + 0.5 * jnp.tanh(logit[:16] + logit[16:])
    weight = dot(weight_pick[...], lifted[:count, :], ((1,), (1,)))
    weight = (weight[:16] + weight[16:]) * scale
    if own is not None:
        gate, weight = gate * own, weight * own
    spread = dot(gate.astype(BF16), messages)
    row = iota((16, 128), 0)
    message_sum = jnp.zeros((16, 128), F32)
    for i in range(16):
        message_sum = message_sum + jnp.where(row == i, spread[:, i * 128 : i * 128 + 128], 0.0)
    coord_sum = [jnp.sum(offsets[k] * weight, axis=1, keepdims=True) for k in range(3)]
    return message_sum, coord_sum


def layer(
    feat_hbm, place_hbm, table_hbm, w_tgt_hbm, w_src_hbm, w_dist_hbm, bias_hbm, w_edge_hbm, w_gate_hbm,
    w_coord_hbm, w_weight_hbm, w_in_hbm, w_out_hbm,
    feat_out, place_out,
    feat, place, table, w_tgt, w_src, w_dist, bias, w_edge, w_gate, w_coord, w_weight, w_in, w_out,
    place_row, near_feat, near_place, plane_feat, plane_place, picked_feat, picked_place,
    column_feat, column_place, lhs, place_list, wide, edge_wide, coord_wide, gate_pick, weight_pick,
    hidden, message, lifted,
    load_sem, send_sem, recv_sem, ready_sem,
):
    blk, edge = lax.axis_index("blk"), lax.axis_index("edge")
    x, y, z_hi = blk // 16, (blk // 2) % 8, blk % 2
    core = edge % 2
    z = z_hi * 4 + edge // 2
    here = x * 8 + y
    spot = z * 2 + core

    plane = [{"blk": (lax.rem(x + dx, NX) * NY + lax.rem(y + dy, NY)) * 2 + z_hi} for dx, dy in PLANE]
    across = [{"blk": here * 2 + 1 - z_hi, "edge": k} for k in range(8)]
    near = [{"edge": lax.rem(edge + step, 8)} for step in EDGE]

    loads = [
        pltpu.make_async_copy(a, b, load_sem.at[k])
        for k, (a, b) in enumerate(
            [
                (feat_hbm, feat), (place_hbm, place), (table_hbm, table), (w_tgt_hbm, w_tgt), (w_src_hbm, w_src),
                (w_dist_hbm, w_dist), (bias_hbm, bias), (w_edge_hbm, w_edge), (w_gate_hbm, w_gate),
                (w_coord_hbm, w_coord), (w_weight_hbm, w_weight), (w_in_hbm, w_in), (w_out_hbm, w_out),
            ]
        )
    ]
    loads[0].start()
    loads[1].start()
    barrier = pltpu.get_barrier_semaphore()
    for peer in plane + near:
        pl.semaphore_signal(barrier, inc=1, device_id=peer, device_id_type=MESH)

    @pl.when(z_hi == 0)
    def _():
        for peer in across:
            pl.semaphore_signal(barrier, inc=1, device_id=peer, device_id_type=MESH)

    loads[0].wait()
    loads[1].wait()
    places = place[...]
    row = jnp.zeros((1, 128), F32)
    for k in range(3):
        row = row + dot(places[k : k + 1], (iota((16, 128), 0) + 16 * k == iota((16, 128), 1)).astype(BF16))
    place_row[...] = row
    pl.semaphore_wait(barrier, len(plane) + len(near) + len(across) * z_hi)

    def send(source, target, k, peer):
        pltpu.make_async_remote_copy(
            source, target, send_sem.at[k], recv_sem.at[k], device_id=peer, device_id_type=MESH
        ).start()

    def wait(buffer, count, semaphore):
        part = buffer.at[pl.ds(0, count)]
        pltpu.make_async_copy(part, part, semaphore).wait()

    for peer in plane:
        send(feat, plane_feat.at[here], 0, peer)
        send(place_row, plane_place.at[here], 1, peer)
    @pl.when(z_hi == 1)
    def _():
        for peer in across:
            pl.semaphore_signal(ready_sem, inc=1, device_id=peer, device_id_type=MESH)

    for copy in loads[2:]:
        copy.start()
    for peer in near:
        send(feat, near_feat.at[edge], 2, peer)
        send(place_row, near_place.at[edge], 3, peer)
    plane_feat[here] = feat[...]
    plane_place[here] = row
    near_feat[edge] = feat[...]
    near_place[edge] = row

    for copy in loads[2:]:
        copy.wait()
    own_feat = feat[...]
    cols = [
        dot(places, (iota((3, 128), 0) == k).astype(BF16), ((0,), (0,))) for k in range(3)
    ]
    own_norm = cols[0] * cols[0] + cols[1] * cols[1] + cols[2] * cols[2]
    dist = w_dist[...]
    base = 0.5 * (dot(own_feat, w_tgt[...]) + bias[...] + own_norm * dist)
    cross = [split2(-c * dist) for c in cols]
    dist_high, dist_mid = split2(jnp.broadcast_to(0.5 * dist, (16, 128)))
    base_high, base_mid = split2(base)
    stack = [c[0] for c in cross] + [c[1] for c in cross]
    stack += [dist_high] * 3 + [dist_mid] * 3 + [dist_high] * 3 + [base_high, base_mid]
    stack = jnp.concatenate(stack + [jnp.zeros((16, 128), BF16)] * (TERMS - len(stack)), axis=0)
    to, of = iota((512, 512), 0), iota((512, 512), 1)
    turned = dot((of == (to % TERMS) * 16 + to // TERMS).astype(BF16), stack).astype(BF16)
    src_half = w_src[...] * jnp.asarray(0.5, BF16)
    none = jnp.zeros((128, 128), BF16)
    for pair in range(8):
        wide[pair, :128, :128] = src_half
        wide[pair, :128, 128:] = src_half
        for side in range(2):
            at = (2 * pair + side) * TERMS
            wide[pair, 128 : 128 + TERMS, side * 128 : side * 128 + 128] = turned[at : at + TERMS]
        wide[pair, 128 + TERMS :, :] = jnp.zeros((128 - TERMS, 256), BF16)
    for full, part in ((edge_wide, w_edge), (coord_wide, w_coord)):
        halved = part[...] * jnp.asarray(0.5, BF16)
        full[:128, :128] = halved
        full[128:, 128:] = halved
        full[:128, 128:] = none
        full[128:, :128] = none

    mine = iota((16, 2048), 0) == iota((16, 2048), 1) // 128
    for pick, vector in ((gate_pick, 0.5 * w_gate[...]), (weight_pick, w_weight[...])):
        for side, part in enumerate(split2(vector)):
            part = jnp.concatenate([part.astype(F32)] * 16, axis=1)
            pick[side * 16 : side * 16 + 16, :] = jnp.where(mine, part, 0.0).astype(BF16)
    shared = (cols, wide, edge_wide[...], coord_wide[...], gate_pick, weight_pick, hidden, message, lifted)

    wait(plane_feat, 31, recv_sem.at[0])
    wait(plane_place, 31, recv_sem.at[1])
    for side in range(2):
        for r in range(3):
            from_spot = table[r, here * 2 + side] // 2
            picked_feat[side, r] = plane_feat[from_spot]
            picked_place[side, r] = plane_place[from_spot]
    for to in range(16):
        if to == 8:

            @pl.when(z_hi == 0)
            def _():
                pl.semaphore_wait(ready_sem, 8)

        @pl.when(spot != to)
        def _(to=to):
            peer = {"blk": here * 2 + to // 8, "edge": to % 8}
            send(picked_feat.at[to // 8], column_feat.at[spot], 4, peer)
            send(picked_place.at[to // 8], column_place.at[spot], 5, peer)
    column_feat[spot] = picked_feat[z_hi]
    column_place[spot] = picked_place[z_hi]
    wait(near_feat, 7, recv_sem.at[2])
    wait(near_place, 7, recv_sem.at[3])
    for k in range(8):
        place_list[k : k + 1, :] = near_place[k]
    keep = (iota((16, 128), 1) != edge * 16 + iota((16, 128), 0)).astype(F32)
    near_rows = lambda at: near_feat[...].reshape(128, 128)
    message_own, coord_own = edge_sums(near_rows, place_list[0:8, :], 128, keep, *shared)

    wait(column_feat, 15, recv_sem.at[4])
    wait(column_place, 15, recv_sem.at[5])
    for r in range(3):
        side = table[r, blk] % 2
        for k in range(8):
            at = r * 8 + k
            lhs[at * 16 : at * 16 + 16, :] = column_feat[side * 8 + k, r]
            place_list[at : at + 1, :] = column_place[side * 8 + k, r]
    far_rows = lambda at: lhs[at : at + 128, :]
    message_far, coord_far = edge_sums(far_rows, place_list[...], 384, None, *shared)

    mean_scale = 1.0 / 511
    mean = ((message_own + message_far) * mean_scale).astype(BF16)
    node_pre = dot(own_feat, w_in[:128, :]) + dot(mean, w_in[128:, :])
    node_hidden = (node_pre * jax.nn.sigmoid(node_pre)).astype(BF16)
    feat_out[...] = (own_feat.astype(F32) + dot(node_hidden, w_out[...])).astype(BF16)
    eye = iota((16, 16), 0) == iota((16, 16), 1)
    for k in range(3):
        moved = jnp.sum(jnp.where(eye, coord_own[k] + coord_far[k], 0.0), axis=0, keepdims=True)
        place_out[k : k + 1, :] = places[k : k + 1].astype(F32) + mean_scale * moved

    for k, buffer, count in (
        (0, plane_feat, 31), (1, plane_place, 31), (2, near_feat, 7), (3, near_place, 7),
        (4, column_feat, 15), (5, column_place, 15),
    ):
        wait(buffer, count, send_sem.at[k])


def deliver(feat_in, place_in, feat_out, place_out, sems):
    copies = [
        pltpu.make_async_copy(feat_in, feat_out, sems.at[0]),
        pltpu.make_async_copy(place_in, place_out, sems.at[1]),
    ]
    for copy in copies:
        copy.start()
    for copy in copies:
        copy.wait()


def shards(*args):
    args = [a.reshape(1, -1) if a.ndim == 1 else a for a in args]
    vmem = lambda shape, kind: pltpu.VMEM(shape, kind)
    loaded = [
        pltpu.SMEM(a.shape, a.dtype) if a.dtype == jnp.int32 else pltpu.VMEM(a.shape, a.dtype) for a in args
    ]
    args = [pltpu.with_memory_space_constraint(a, pltpu.HBM) for a in args]
    results = pl.pallas_call(
        layer,
        out_shape=(pltpu.VMEM((ROWS, 128), BF16), pltpu.VMEM((3, ROWS), F32)),
        in_specs=[pl.BlockSpec(memory_space=pltpu.HBM)] * len(args),
        out_specs=(pl.BlockSpec(memory_space=pltpu.VMEM), pl.BlockSpec(memory_space=pltpu.VMEM)),
        scratch_shapes=loaded
        + [
            vmem((1, 128), F32),
            vmem((8, 16, 128), BF16),
            vmem((8, 1, 128), F32),
            vmem((32, 16, 128), BF16),
            vmem((32, 1, 128), F32),
            vmem((2, 3, 16, 128), BF16),
            vmem((2, 3, 1, 128), F32),
            vmem((16, 3, 16, 128), BF16),
            vmem((16, 3, 1, 128), F32),
            vmem((384, 128), BF16),
            vmem((24, 128), F32),
            vmem((8, 256, 256), BF16),
            vmem((256, 256), BF16),
            vmem((256, 256), BF16),
            vmem((32, 2048), BF16),
            vmem((32, 2048), BF16),
            vmem((384, 2048), BF16),
            vmem((384, 2048), BF16),
            vmem((384, 2048), BF16),
            pltpu.SemaphoreType.DMA((13,)),
            pltpu.SemaphoreType.DMA((6,)),
            pltpu.SemaphoreType.DMA((6,)),
            pltpu.SemaphoreType.REGULAR,
        ],
        compiler_params=pltpu.CompilerParams(
            collective_id=0, has_side_effects=True, vmem_limit_bytes=40 * 1024 * 1024
        ),
    )(*args)
    return pl.pallas_call(
        deliver,
        out_shape=(jax.ShapeDtypeStruct((ROWS, 128), BF16), jax.ShapeDtypeStruct((3, ROWS), F32)),
        in_specs=[pl.BlockSpec(memory_space=pltpu.VMEM)] * 2,
        out_specs=(pl.BlockSpec(memory_space=pltpu.HBM),) * 2,
        scratch_shapes=[pltpu.SemaphoreType.DMA((2,))],
    )(*[pltpu.with_memory_space_constraint(r, pltpu.VMEM) for r in results])


def solution(mesh):
    specs = (P(("blk", "edge"), None), P(None, ("blk", "edge"))) + (P(),) * 11
    return jax.shard_map(
        shards,
        mesh=mesh,
        in_specs=specs,
        out_specs=(P(("blk", "edge"), None), P(None, ("blk", "edge"))),
        check_vma=False,
    )
```

```python
import functools

import jax
import jax.numpy as jnp
from jax import lax
from jax.experimental import pallas as pl
from jax.experimental.pallas import tpu as pltpu
from jax.sharding import PartitionSpec as P

MESH = pl.DeviceIdType.MESH
F32 = jnp.float32
BF16 = jnp.bfloat16

NX, NY, NZ = 4, 8, 8
RING = {4: (2, 1, 3, 0), 8: (4, 3, 5, 2, 6, 1, 7, 0)}
PLANE = [(dx, dy) for dx in RING[NX] for dy in RING[NY] if dx or dy]
EDGE = (4, 3, 5, 2, 6, 1, 7)
ROWS = 16
TERMS = 32


def iota(shape, dim):
    return lax.broadcasted_iota(jnp.int32, shape, dim)


def dot(a, b, dims=((1,), (0,))):
    return lax.dot_general(a, b, (dims, ((), ())), preferred_element_type=F32)


def split2(a):
    high = a.astype(BF16)
    return high, (a - high.astype(F32)).astype(BF16)


def half_silu(h):
    return h + h * jnp.tanh(h)


def place_terms(places, count):
    slots = places.shape[0]
    spread = jnp.broadcast_to(places[:, None, :], (slots, 16, 128)).reshape(count, 128)
    lane, node = iota((count, 128), 1), lax.rem(iota((count, 128), 0), 16)
    spread = jnp.where(lax.rem(lane, 16) == node, spread, 0.0)
    square_high, square_low = split2(spread * spread)
    parts = jnp.concatenate([spread.astype(BF16), square_high, square_low], axis=1)
    row, term = iota((384, 128), 0), iota((384, 128), 1)
    axis = lax.rem(row, 128) // 16
    kind = row // 128
    first = jnp.where(kind == 0, 0, 6 * kind)
    hit = (term == first + axis) | ((kind < 2) & (term == first + 3 + axis))
    placed = dot(parts, ((axis < 3) & hit).astype(BF16))
    ones = (lane == 15) | (lane == 16)
    return jnp.where(ones, 1.0, placed).astype(BF16)


def edge_sums(feats, places, count, own, target_cols, wide, w_edge2, w_coord2, gate_pick, weight_pick, hidden, message, lifted):
    terms = place_terms(places, count)
    chunks = [(at, pair) for pair in range(8) for at in range(0, count, 128)]
    lhs = [jnp.concatenate([feats(at), terms[at : at + 128]], axis=1) for at in range(0, count, 128)]
    for at, pair in chunks:
        half = dot(lhs[at // 128], wide[pair]).astype(BF16)
        hidden[at : at + 128, pair * 256 : pair * 256 + 256] = half_silu(half)

    rows8 = dot((iota((8, 128), 0) == iota((8, 128), 1)).astype(BF16), terms, ((1,), (1,)))
    offsets = [target_cols[k][:, :1] - rows8[k : k + 1] for k in range(3)]
    radial = offsets[0] * offsets[0] + offsets[1] * offsets[1] + offsets[2] * offsets[2]
    scale = 1.0 / (jnp.sqrt(radial) + 1.0)

    for at, pair in chunks:
        half = dot(hidden[at : at + 128, pair * 256 : pair * 256 + 256], w_edge2).astype(BF16)
        message[at : at + 128, pair * 256 : pair * 256 + 256] = half_silu(half)
    for at, pair in chunks:
        half = dot(message[at : at + 128, pair * 256 : pair * 256 + 256], w_coord2).astype(BF16)
        lifted[at : at + 128, pair * 256 : pair * 256 + 256] = half_silu(half)
    messages = message[:count, :]
    logit = dot(gate_pick[...], messages, ((1,), (1,)))
    gate = 0.5 + 0.5 * jnp.tanh(logit[:16] + logit[16:])
    weight = dot(weight_pick[...], lifted[:count, :], ((1,), (1,)))
    weight = (weight[:16] + weight[16:]) * scale
    if own is not None:
        gate, weight = gate * own, weight * own
    spread = dot(gate.astype(BF16), messages)
    row = iota((16, 128), 0)
    message_sum = jnp.zeros((16, 128), F32)
    for i in range(16):
        message_sum = message_sum + jnp.where(row == i, spread[:, i * 128 : i * 128 + 128], 0.0)
    coord_sum = [jnp.sum(offsets[k] * weight, axis=1, keepdims=True) for k in range(3)]
    return message_sum, coord_sum


def layer(
    feat_hbm, place_hbm, table_hbm, w_tgt_hbm, w_src_hbm, w_dist_hbm, bias_hbm, w_edge_hbm, w_gate_hbm,
    w_coord_hbm, w_weight_hbm, w_in_hbm, w_out_hbm,
    feat_out, place_out,
    feat, place, table, w_tgt, w_src, w_dist, bias, w_edge, w_gate, w_coord, w_weight, w_in, w_out,
    place_row, near_feat, near_place, plane_feat, plane_place, picked_feat, picked_place,
    column_feat, column_place, lhs, place_list, wide, edge_wide, coord_wide, gate_pick, weight_pick,
    hidden, message, lifted,
    load_sem, send_sem, recv_sem, ready_sem,
):
    blk, edge = lax.axis_index("blk"), lax.axis_index("edge")
    x, y, z_hi = blk // 16, (blk // 2) % 8, blk % 2
    core = edge % 2
    z = z_hi * 4 + edge // 2
    here = x * 8 + y
    spot = z * 2 + core

    plane = [{"blk": (lax.rem(x + dx, NX) * NY + lax.rem(y + dy, NY)) * 2 + z_hi} for dx, dy in PLANE]
    across = [{"blk": here * 2 + 1 - z_hi, "edge": k} for k in range(8)]
    near = [{"edge": lax.rem(edge + step, 8)} for step in EDGE]

    loads = [
        pltpu.make_async_copy(a, b, load_sem.at[k])
        for k, (a, b) in enumerate(
            [
                (feat_hbm, feat), (place_hbm, place), (table_hbm, table), (w_tgt_hbm, w_tgt), (w_src_hbm, w_src),
                (w_dist_hbm, w_dist), (bias_hbm, bias), (w_edge_hbm, w_edge), (w_gate_hbm, w_gate),
                (w_coord_hbm, w_coord), (w_weight_hbm, w_weight), (w_in_hbm, w_in), (w_out_hbm, w_out),
            ]
        )
    ]
    loads[0].start()
    loads[1].start()
    barrier = pltpu.get_barrier_semaphore()
    for peer in plane + near:
        pl.semaphore_signal(barrier, inc=1, device_id=peer, device_id_type=MESH)

    @pl.when(z_hi == 0)
    def _():
        for peer in across:
            pl.semaphore_signal(barrier, inc=1, device_id=peer, device_id_type=MESH)

    loads[0].wait()
    loads[1].wait()
    places = place[...]
    row = jnp.zeros((1, 128), F32)
    for k in range(3):
        row = row + dot(places[k : k + 1], (iota((16, 128), 0) + 16 * k == iota((16, 128), 1)).astype(BF16))
    place_row[...] = row
    pl.semaphore_wait(barrier, len(plane) + len(near) + len(across) * z_hi)

    def send(source, target, k, peer):
        pltpu.make_async_remote_copy(
            source, target, send_sem.at[k], recv_sem.at[k], device_id=peer, device_id_type=MESH
        ).start()

    def wait(buffer, count, semaphore):
        part = buffer.at[pl.ds(0, count)]
        pltpu.make_async_copy(part, part, semaphore).wait()

    for px, py in sorted(((a, b) for a in range(NX) for b in range(NY)), key=lambda q: min(q[0], NX - q[0]) + min(q[1], NY - q[1])):

        @pl.when(here != px * NY + py)
        def _(px=px, py=py):
            peer = {"blk": (px * NY + py) * 2 + z_hi}
            send(feat, plane_feat.at[here], 0, peer)
            send(place_row, plane_place.at[here], 1, peer)

    @pl.when(z_hi == 1)
    def _():
        for peer in across:
            pl.semaphore_signal(ready_sem, inc=1, device_id=peer, device_id_type=MESH)

    for copy in loads[2:]:
        copy.start()
    for peer in near:
        send(feat, near_feat.at[edge], 2, peer)
        send(place_row, near_place.at[edge], 3, peer)
    plane_feat[here] = feat[...]
    plane_place[here] = row
    near_feat[edge] = feat[...]
    near_place[edge] = row

    for copy in loads[2:]:
        copy.wait()
    own_feat = feat[...]
    cols = [
        dot(places, (iota((3, 128), 0) == k).astype(BF16), ((0,), (0,))) for k in range(3)
    ]
    own_norm = cols[0] * cols[0] + cols[1] * cols[1] + cols[2] * cols[2]
    dist = w_dist[...]
    base = 0.5 * (dot(own_feat, w_tgt[...]) + bias[...] + own_norm * dist)
    cross = [split2(-c * dist) for c in cols]
    dist_high, dist_mid = split2(jnp.broadcast_to(0.5 * dist, (16, 128)))
    base_high, base_mid = split2(base)
    stack = [c[0] for c in cross] + [c[1] for c in cross]
    stack += [dist_high] * 3 + [dist_mid] * 3 + [dist_high] * 3 + [base_high, base_mid]
    stack = jnp.concatenate(stack + [jnp.zeros((16, 128), BF16)] * (TERMS - len(stack)), axis=0)
    to, of = iota((512, 512), 0), iota((512, 512), 1)
    turned = dot((of == (to % TERMS) * 16 + to // TERMS).astype(BF16), stack).astype(BF16)
    src_half = w_src[...] * jnp.asarray(0.5, BF16)
    none = jnp.zeros((128, 128), BF16)
    for pair in range(8):
        wide[pair, :128, :128] = src_half
        wide[pair, :128, 128:] = src_half
        for side in range(2):
            at = (2 * pair + side) * TERMS
            wide[pair, 128 : 128 + TERMS, side * 128 : side * 128 + 128] = turned[at : at + TERMS]
        wide[pair, 128 + TERMS :, :] = jnp.zeros((128 - TERMS, 256), BF16)
    for full, part in ((edge_wide, w_edge), (coord_wide, w_coord)):
        halved = part[...] * jnp.asarray(0.5, BF16)
        full[:128, :128] = halved
        full[128:, 128:] = halved
        full[:128, 128:] = none
        full[128:, :128] = none

    mine = iota((16, 2048), 0) == iota((16, 2048), 1) // 128
    for pick, vector in ((gate_pick, 0.5 * w_gate[...]), (weight_pick, w_weight[...])):
        for side, part in enumerate(split2(vector)):
            part = jnp.concatenate([part.astype(F32)] * 16, axis=1)
            pick[side * 16 : side * 16 + 16, :] = jnp.where(mine, part, 0.0).astype(BF16)
    shared = (cols, wide, edge_wide[...], coord_wide[...], gate_pick, weight_pick, hidden, message, lifted)

    wait(plane_feat, 31, recv_sem.at[0])
    wait(plane_place, 31, recv_sem.at[1])
    for side in range(2):
        for r in range(3):
            from_spot = table[r, here * 2 + side] // 2
            picked_feat[side, r] = plane_feat[from_spot]
            picked_place[side, r] = plane_place[from_spot]
    for to in range(16):
        if to == 8:

            @pl.when(z_hi == 0)
            def _():
                pl.semaphore_wait(ready_sem, 8)

        @pl.when(spot != to)
        def _(to=to):
            peer = {"blk": here * 2 + to // 8, "edge": to % 8}
            send(picked_feat.at[to // 8], column_feat.at[spot], 4, peer)
            send(picked_place.at[to // 8], column_place.at[spot], 5, peer)
    column_feat[spot] = picked_feat[z_hi]
    column_place[spot] = picked_place[z_hi]
    wait(near_feat, 7, recv_sem.at[2])
    wait(near_place, 7, recv_sem.at[3])
    for k in range(8):
        place_list[k : k + 1, :] = near_place[k]
    keep = (iota((16, 128), 1) != edge * 16 + iota((16, 128), 0)).astype(F32)
    near_rows = lambda at: near_feat[...].reshape(128, 128)
    message_own, coord_own = edge_sums(near_rows, place_list[0:8, :], 128, keep, *shared)

    wait(column_feat, 15, recv_sem.at[4])
    wait(column_place, 15, recv_sem.at[5])
    for r in range(3):
        side = table[r, blk] % 2
        for k in range(8):
            at = r * 8 + k
            lhs[at * 16 : at * 16 + 16, :] = column_feat[side * 8 + k, r]
            place_list[at : at + 1, :] = column_place[side * 8 + k, r]
    far_rows = lambda at: lhs[at : at + 128, :]
    message_far, coord_far = edge_sums(far_rows, place_list[...], 384, None, *shared)

    mean_scale = 1.0 / 511
    mean = ((message_own + message_far) * mean_scale).astype(BF16)
    node_pre = dot(own_feat, w_in[:128, :]) + dot(mean, w_in[128:, :])
    node_hidden = (node_pre * jax.nn.sigmoid(node_pre)).astype(BF16)
    feat_out[...] = (own_feat.astype(F32) + dot(node_hidden, w_out[...])).astype(BF16)
    eye = iota((16, 16), 0) == iota((16, 16), 1)
    for k in range(3):
        moved = jnp.sum(jnp.where(eye, coord_own[k] + coord_far[k], 0.0), axis=0, keepdims=True)
        place_out[k : k + 1, :] = places[k : k + 1].astype(F32) + mean_scale * moved

    for k, buffer, count in (
        (0, plane_feat, 31), (1, plane_place, 31), (2, near_feat, 7), (3, near_place, 7),
        (4, column_feat, 15), (5, column_place, 15),
    ):
        wait(buffer, count, send_sem.at[k])


def deliver(feat_in, place_in, feat_out, place_out, sems):
    copies = [
        pltpu.make_async_copy(feat_in, feat_out, sems.at[0]),
        pltpu.make_async_copy(place_in, place_out, sems.at[1]),
    ]
    for copy in copies:
        copy.start()
    for copy in copies:
        copy.wait()


def shards(*args):
    args = [a.reshape(1, -1) if a.ndim == 1 else a for a in args]
    vmem = lambda shape, kind: pltpu.VMEM(shape, kind)
    loaded = [
        pltpu.SMEM(a.shape, a.dtype) if a.dtype == jnp.int32 else pltpu.VMEM(a.shape, a.dtype) for a in args
    ]
    args = [pltpu.with_memory_space_constraint(a, pltpu.HBM) for a in args]
    results = pl.pallas_call(
        layer,
        out_shape=(pltpu.VMEM((ROWS, 128), BF16), pltpu.VMEM((3, ROWS), F32)),
        in_specs=[pl.BlockSpec(memory_space=pltpu.HBM)] * len(args),
        out_specs=(pl.BlockSpec(memory_space=pltpu.VMEM), pl.BlockSpec(memory_space=pltpu.VMEM)),
        scratch_shapes=loaded
        + [
            vmem((1, 128), F32),
            vmem((8, 16, 128), BF16),
            vmem((8, 1, 128), F32),
            vmem((32, 16, 128), BF16),
            vmem((32, 1, 128), F32),
            vmem((2, 3, 16, 128), BF16),
            vmem((2, 3, 1, 128), F32),
            vmem((16, 3, 16, 128), BF16),
            vmem((16, 3, 1, 128), F32),
            vmem((384, 128), BF16),
            vmem((24, 128), F32),
            vmem((8, 256, 256), BF16),
            vmem((256, 256), BF16),
            vmem((256, 256), BF16),
            vmem((32, 2048), BF16),
            vmem((32, 2048), BF16),
            vmem((384, 2048), BF16),
            vmem((384, 2048), BF16),
            vmem((384, 2048), BF16),
            pltpu.SemaphoreType.DMA((13,)),
            pltpu.SemaphoreType.DMA((6,)),
            pltpu.SemaphoreType.DMA((6,)),
            pltpu.SemaphoreType.REGULAR,
        ],
        compiler_params=pltpu.CompilerParams(
            collective_id=0, has_side_effects=True, vmem_limit_bytes=40 * 1024 * 1024
        ),
    )(*args)
    return pl.pallas_call(
        deliver,
        out_shape=(jax.ShapeDtypeStruct((ROWS, 128), BF16), jax.ShapeDtypeStruct((3, ROWS), F32)),
        in_specs=[pl.BlockSpec(memory_space=pltpu.VMEM)] * 2,
        out_specs=(pl.BlockSpec(memory_space=pltpu.HBM),) * 2,
        scratch_shapes=[pltpu.SemaphoreType.DMA((2,))],
    )(*[pltpu.with_memory_space_constraint(r, pltpu.VMEM) for r in results])


def solution(mesh):
    specs = (P(("blk", "edge"), None), P(None, ("blk", "edge"))) + (P(),) * 11
    return jax.shard_map(
        shards,
        mesh=mesh,
        in_specs=specs,
        out_specs=(P(("blk", "edge"), None), P(None, ("blk", "edge"))),
        check_vma=False,
    )
```

```python
import functools

import jax
import jax.numpy as jnp
from jax import lax
from jax.experimental import pallas as pl
from jax.experimental.pallas import tpu as pltpu
from jax.sharding import PartitionSpec as P

MESH = pl.DeviceIdType.MESH
F32 = jnp.float32
BF16 = jnp.bfloat16

NX, NY, NZ = 4, 8, 8
RING = {4: (2, 1, 3, 0), 8: (4, 3, 5, 2, 6, 1, 7, 0)}
PLANE = [(dx, dy) for dx in RING[NX] for dy in RING[NY] if dx or dy]
EDGE = (4, 3, 5, 2, 6, 1, 7)
ROWS = 16
TERMS = 32


def iota(shape, dim):
    return lax.broadcasted_iota(jnp.int32, shape, dim)


def dot(a, b, dims=((1,), (0,))):
    return lax.dot_general(a, b, (dims, ((), ())), preferred_element_type=F32)


def split2(a):
    high = a.astype(BF16)
    return high, (a - high.astype(F32)).astype(BF16)


def half_silu(h):
    return h + h * jnp.tanh(h)


def place_terms(places, count):
    slots = places.shape[0]
    spread = jnp.broadcast_to(places[:, None, :], (slots, 16, 128)).reshape(count, 128)
    lane, node = iota((count, 128), 1), lax.rem(iota((count, 128), 0), 16)
    spread = jnp.where(lax.rem(lane, 16) == node, spread, 0.0)
    square_high, square_low = split2(spread * spread)
    parts = jnp.concatenate([spread.astype(BF16), square_high, square_low], axis=1)
    row, term = iota((384, 128), 0), iota((384, 128), 1)
    axis = lax.rem(row, 128) // 16
    kind = row // 128
    first = jnp.where(kind == 0, 0, 6 * kind)
    hit = (term == first + axis) | ((kind < 2) & (term == first + 3 + axis))
    placed = dot(parts, ((axis < 3) & hit).astype(BF16))
    ones = (lane == 15) | (lane == 16)
    return jnp.where(ones, 1.0, placed).astype(BF16)


def edge_sums(feats, places, count, own, target_cols, wide, w_edge2, w_coord2, gate_pick, weight_pick, hidden, message, lifted):
    terms = place_terms(places, count)
    chunks = [(at, pair) for pair in range(8) for at in range(0, count, 128)]
    lhs = [jnp.concatenate([feats(at), terms[at : at + 128]], axis=1) for at in range(0, count, 128)]
    for at, pair in chunks:
        half = dot(lhs[at // 128], wide[pair]).astype(BF16)
        hidden[at : at + 128, pair * 256 : pair * 256 + 256] = half_silu(half)

    rows8 = dot((iota((8, 128), 0) == iota((8, 128), 1)).astype(BF16), terms, ((1,), (1,)))
    offsets = [target_cols[k][:, :1] - rows8[k : k + 1] for k in range(3)]
    radial = offsets[0] * offsets[0] + offsets[1] * offsets[1] + offsets[2] * offsets[2]
    scale = 1.0 / (jnp.sqrt(radial) + 1.0)

    for at, pair in chunks:
        half = dot(hidden[at : at + 128, pair * 256 : pair * 256 + 256], w_edge2).astype(BF16)
        message[at : at + 128, pair * 256 : pair * 256 + 256] = half_silu(half)
    for at, pair in chunks:
        half = dot(message[at : at + 128, pair * 256 : pair * 256 + 256], w_coord2).astype(BF16)
        lifted[at : at + 128, pair * 256 : pair * 256 + 256] = half_silu(half)
    messages = message[:count, :]
    logit = dot(gate_pick[...], messages, ((1,), (1,)))
    gate = 0.5 + 0.5 * jnp.tanh(logit[:16] + logit[16:])
    weight = dot(weight_pick[...], lifted[:count, :], ((1,), (1,)))
    weight = (weight[:16] + weight[16:]) * scale
    if own is not None:
        gate, weight = gate * own, weight * own
    spread = dot(gate.astype(BF16), messages)
    row = iota((16, 128), 0)
    message_sum = jnp.zeros((16, 128), F32)
    for i in range(16):
        message_sum = message_sum + jnp.where(row == i, spread[:, i * 128 : i * 128 + 128], 0.0)
    coord_sum = [jnp.sum(offsets[k] * weight, axis=1, keepdims=True) for k in range(3)]
    return message_sum, coord_sum


def layer(
    feat_hbm, place_hbm, table_hbm, w_tgt_hbm, w_src_hbm, w_dist_hbm, bias_hbm, w_edge_hbm, w_gate_hbm,
    w_coord_hbm, w_weight_hbm, w_in_hbm, w_out_hbm,
    feat_out, place_out,
    feat, place, table, w_tgt, w_src, w_dist, bias, w_edge, w_gate, w_coord, w_weight, w_in, w_out,
    place_row, near_feat, near_place, plane_feat, plane_place, picked_feat, picked_place,
    column_feat, column_place, lhs, place_list, wide, edge_wide, coord_wide, gate_pick, weight_pick,
    hidden, message, lifted,
    load_sem, send_sem, recv_sem, ready_sem,
):
    blk, edge = lax.axis_index("blk"), lax.axis_index("edge")
    x, y, z_hi = blk // 16, (blk // 2) % 8, blk % 2
    core = edge % 2
    z = z_hi * 4 + edge // 2
    here = x * 8 + y
    spot = z * 2 + core

    plane = [{"blk": (lax.rem(x + dx, NX) * NY + lax.rem(y + dy, NY)) * 2 + z_hi} for dx, dy in PLANE]
    across = [{"blk": here * 2 + 1 - z_hi, "edge": k} for k in range(8)]
    near = [{"edge": lax.rem(edge + step, 8)} for step in EDGE]

    loads = [
        pltpu.make_async_copy(a, b, load_sem.at[k])
        for k, (a, b) in enumerate(
            [
                (feat_hbm, feat), (place_hbm, place), (table_hbm, table), (w_tgt_hbm, w_tgt), (w_src_hbm, w_src),
                (w_dist_hbm, w_dist), (bias_hbm, bias), (w_edge_hbm, w_edge), (w_gate_hbm, w_gate),
                (w_coord_hbm, w_coord), (w_weight_hbm, w_weight), (w_in_hbm, w_in), (w_out_hbm, w_out),
            ]
        )
    ]
    loads[0].start()
    loads[1].start()
    barrier = pltpu.get_barrier_semaphore()
    for peer in plane + near:
        pl.semaphore_signal(barrier, inc=1, device_id=peer, device_id_type=MESH)

    @pl.when(z_hi == 0)
    def _():
        for peer in across:
            pl.semaphore_signal(barrier, inc=1, device_id=peer, device_id_type=MESH)

    loads[0].wait()
    loads[1].wait()
    places = place[...]
    row = jnp.zeros((1, 128), F32)
    for k in range(3):
        row = row + dot(places[k : k + 1], (iota((16, 128), 0) + 16 * k == iota((16, 128), 1)).astype(BF16))
    place_row[...] = row
    pl.semaphore_wait(barrier, len(plane) + len(near) + len(across) * z_hi)

    def send(source, target, k, peer):
        pltpu.make_async_remote_copy(
            source, target, send_sem.at[k], recv_sem.at[k], device_id=peer, device_id_type=MESH
        ).start()

    def wait(buffer, count, semaphore):
        part = buffer.at[pl.ds(0, count)]
        pltpu.make_async_copy(part, part, semaphore).wait()

    for px, py in sorted(((a, b) for a in range(NX) for b in range(NY)), key=lambda q: min(q[0], NX - q[0]) + min(q[1], NY - q[1])):

        @pl.when(here != px * NY + py)
        def _(px=px, py=py):
            peer = {"blk": (px * NY + py) * 2 + z_hi}
            send(feat, plane_feat.at[here], 0, peer)
            send(place_row, plane_place.at[here], 1, peer)

    @pl.when(z_hi == 1)
    def _():
        for peer in across:
            pl.semaphore_signal(ready_sem, inc=1, device_id=peer, device_id_type=MESH)

    for copy in loads[2:]:
        copy.start()
    for peer in near:
        send(feat, near_feat.at[edge], 2, peer)
        send(place_row, near_place.at[edge], 3, peer)
    plane_feat[here] = feat[...]
    plane_place[here] = row
    near_feat[edge] = feat[...]
    near_place[edge] = row

    for copy in loads[2:]:
        copy.wait()
    own_feat = feat[...]
    cols = [
        dot(places, (iota((3, 128), 0) == k).astype(BF16), ((0,), (0,))) for k in range(3)
    ]
    own_norm = cols[0] * cols[0] + cols[1] * cols[1] + cols[2] * cols[2]
    dist = w_dist[...]
    base = 0.5 * (dot(own_feat, w_tgt[...]) + bias[...] + own_norm * dist)
    cross = [split2(-c * dist) for c in cols]
    dist_high, dist_mid = split2(jnp.broadcast_to(0.5 * dist, (16, 128)))
    base_high, base_mid = split2(base)
    stack = [c[0] for c in cross] + [c[1] for c in cross]
    stack += [dist_high] * 3 + [dist_mid] * 3 + [dist_high] * 3 + [base_high, base_mid]
    stack = jnp.concatenate(stack + [jnp.zeros((16, 128), BF16)] * (TERMS - len(stack)), axis=0)
    to, of = iota((512, 512), 0), iota((512, 512), 1)
    turned = dot((of == (to % TERMS) * 16 + to // TERMS).astype(BF16), stack).astype(BF16)
    src_half = w_src[...] * jnp.asarray(0.5, BF16)
    none = jnp.zeros((128, 128), BF16)
    for pair in range(8):
        wide[pair, :128, :128] = src_half
        wide[pair, :128, 128:] = src_half
        for side in range(2):
            at = (2 * pair + side) * TERMS
            wide[pair, 128 : 128 + TERMS, side * 128 : side * 128 + 128] = turned[at : at + TERMS]
        wide[pair, 128 + TERMS :, :] = jnp.zeros((128 - TERMS, 256), BF16)
    for full, part in ((edge_wide, w_edge), (coord_wide, w_coord)):
        halved = part[...] * jnp.asarray(0.5, BF16)
        full[:128, :128] = halved
        full[128:, 128:] = halved
        full[:128, 128:] = none
        full[128:, :128] = none

    mine = iota((16, 2048), 0) == iota((16, 2048), 1) // 128
    for pick, vector in ((gate_pick, 0.5 * w_gate[...]), (weight_pick, w_weight[...])):
        for side, part in enumerate(split2(vector)):
            part = jnp.concatenate([part.astype(F32)] * 16, axis=1)
            pick[side * 16 : side * 16 + 16, :] = jnp.where(mine, part, 0.0).astype(BF16)
    shared = (cols, wide, edge_wide[...], coord_wide[...], gate_pick, weight_pick, hidden, message, lifted)

    wait(plane_feat, 31, recv_sem.at[0])
    wait(plane_place, 31, recv_sem.at[1])
    for side in range(2):
        for r in range(3):
            from_spot = table[r, here * 2 + side] // 2
            picked_feat[side, r] = plane_feat[from_spot]
            picked_place[side, r] = plane_place[from_spot]
    for to in [k ^ 1 for k in range(16)]:
        if to == 9:

            @pl.when(z_hi == 0)
            def _():
                pl.semaphore_wait(ready_sem, 8)

        @pl.when(spot != to)
        def _(to=to):
            peer = {"blk": here * 2 + to // 8, "edge": to % 8}
            send(picked_feat.at[to // 8], column_feat.at[spot], 4, peer)
            send(picked_place.at[to // 8], column_place.at[spot], 5, peer)
    column_feat[spot] = picked_feat[z_hi]
    column_place[spot] = picked_place[z_hi]
    wait(near_feat, 7, recv_sem.at[2])
    wait(near_place, 7, recv_sem.at[3])
    for k in range(8):
        place_list[k : k + 1, :] = near_place[k]
    keep = (iota((16, 128), 1) != edge * 16 + iota((16, 128), 0)).astype(F32)
    near_rows = lambda at: near_feat[...].reshape(128, 128)
    message_own, coord_own = edge_sums(near_rows, place_list[0:8, :], 128, keep, *shared)

    wait(column_feat, 15, recv_sem.at[4])
    wait(column_place, 15, recv_sem.at[5])
    for r in range(3):
        side = table[r, blk] % 2
        for k in range(8):
            at = r * 8 + k
            lhs[at * 16 : at * 16 + 16, :] = column_feat[side * 8 + k, r]
            place_list[at : at + 1, :] = column_place[side * 8 + k, r]
    far_rows = lambda at: lhs[at : at + 128, :]
    message_far, coord_far = edge_sums(far_rows, place_list[...], 384, None, *shared)

    mean_scale = 1.0 / 511
    mean = ((message_own + message_far) * mean_scale).astype(BF16)
    node_pre = dot(own_feat, w_in[:128, :]) + dot(mean, w_in[128:, :])
    node_hidden = (node_pre * jax.nn.sigmoid(node_pre)).astype(BF16)
    feat_out[...] = (own_feat.astype(F32) + dot(node_hidden, w_out[...])).astype(BF16)
    eye = iota((16, 16), 0) == iota((16, 16), 1)
    for k in range(3):
        moved = jnp.sum(jnp.where(eye, coord_own[k] + coord_far[k], 0.0), axis=0, keepdims=True)
        place_out[k : k + 1, :] = places[k : k + 1].astype(F32) + mean_scale * moved

    for k, buffer, count in (
        (0, plane_feat, 31), (1, plane_place, 31), (2, near_feat, 7), (3, near_place, 7),
        (4, column_feat, 15), (5, column_place, 15),
    ):
        wait(buffer, count, send_sem.at[k])


def deliver(feat_in, place_in, feat_out, place_out, sems):
    copies = [
        pltpu.make_async_copy(feat_in, feat_out, sems.at[0]),
        pltpu.make_async_copy(place_in, place_out, sems.at[1]),
    ]
    for copy in copies:
        copy.start()
    for copy in copies:
        copy.wait()


def shards(*args):
    args = [a.reshape(1, -1) if a.ndim == 1 else a for a in args]
    vmem = lambda shape, kind: pltpu.VMEM(shape, kind)
    loaded = [
        pltpu.SMEM(a.shape, a.dtype) if a.dtype == jnp.int32 else pltpu.VMEM(a.shape, a.dtype) for a in args
    ]
    args = [pltpu.with_memory_space_constraint(a, pltpu.HBM) for a in args]
    results = pl.pallas_call(
        layer,
        out_shape=(pltpu.VMEM((ROWS, 128), BF16), pltpu.VMEM((3, ROWS), F32)),
        in_specs=[pl.BlockSpec(memory_space=pltpu.HBM)] * len(args),
        out_specs=(pl.BlockSpec(memory_space=pltpu.VMEM), pl.BlockSpec(memory_space=pltpu.VMEM)),
        scratch_shapes=loaded
        + [
            vmem((1, 128), F32),
            vmem((8, 16, 128), BF16),
            vmem((8, 1, 128), F32),
            vmem((32, 16, 128), BF16),
            vmem((32, 1, 128), F32),
            vmem((2, 3, 16, 128), BF16),
            vmem((2, 3, 1, 128), F32),
            vmem((16, 3, 16, 128), BF16),
            vmem((16, 3, 1, 128), F32),
            vmem((384, 128), BF16),
            vmem((24, 128), F32),
            vmem((8, 256, 256), BF16),
            vmem((256, 256), BF16),
            vmem((256, 256), BF16),
            vmem((32, 2048), BF16),
            vmem((32, 2048), BF16),
            vmem((384, 2048), BF16),
            vmem((384, 2048), BF16),
            vmem((384, 2048), BF16),
            pltpu.SemaphoreType.DMA((13,)),
            pltpu.SemaphoreType.DMA((6,)),
            pltpu.SemaphoreType.DMA((6,)),
            pltpu.SemaphoreType.REGULAR,
        ],
        compiler_params=pltpu.CompilerParams(
            collective_id=0, has_side_effects=True, vmem_limit_bytes=40 * 1024 * 1024
        ),
    )(*args)
    return pl.pallas_call(
        deliver,
        out_shape=(jax.ShapeDtypeStruct((ROWS, 128), BF16), jax.ShapeDtypeStruct((3, ROWS), F32)),
        in_specs=[pl.BlockSpec(memory_space=pltpu.VMEM)] * 2,
        out_specs=(pl.BlockSpec(memory_space=pltpu.HBM),) * 2,
        scratch_shapes=[pltpu.SemaphoreType.DMA((2,))],
    )(*[pltpu.with_memory_space_constraint(r, pltpu.VMEM) for r in results])


def solution(mesh):
    specs = (P(("blk", "edge"), None), P(None, ("blk", "edge"))) + (P(),) * 11
    return jax.shard_map(
        shards,
        mesh=mesh,
        in_specs=specs,
        out_specs=(P(("blk", "edge"), None), P(None, ("blk", "edge"))),
        check_vma=False,
    )
```
